256 devices in a mesh: rows: 32 (over x, y, core), cols: 8 (over z).
Axes of the slice: x: 4, y: 4, z: 8, core: 2. Of those that a mesh axis runs over, the one named last changes fastest.
Arguments:
- vectors: float32 [256, 131072], P('cols', 'rows'), may hold values from -6 to 6
- onsite: float32 [131072], P('rows'), may hold values from -2 to 2
- h_blocks: float32 [1024, 9, 128, 128], P('rows'), may hold values from -0.1875 to 0.1875
- block_cols: int32 [1024, 9], P('rows'), may hold values from 0 to 1023, as said below
- block_counts: int32 [1024], P('rows'), may hold values from 3 to 9, as said below
Outputs:
- filtered: float32 [256, 131072], P('cols', 'rows')
- correlation: float32 [256, 256], P('cols')
The draws below stay inside these ranges and needn't reach their ends.
Inputs may be any that keep to these rules, and one draw needn't show every extreme that they name: `block_cols`: entry k of block row r is (r + o) mod 1024 with -4 <= o <= 4; the offsets o of one block row are distinct, and its first three are 0, 4 and -4. `block_counts`: some block row uses all 9 slots.
All inputs are finite; a program needn't handle non-finite values.
Results may differ from the reference program's by a relative error of at most 0.0003.
Values sent between devices are 32-bit elements; how exact they have to be, the bound alone decides.
No kernel may reach another device: no remote copies, remote signals or barrier semaphores. Data moves between devices by JAX's collectives and lax.ppermute only.
A program may use at most 128 MiB of HBM per device.

```python
import jax
import jax.numpy as jnp
from jax import lax

VCOLS = 256
BLOCK = 128
KMAX = 9
REACH = 4
BR_DEV = 32
NBR = 1024
NROWS = 131072


def draw_block_cols(key, part):
    key = jax.random.fold_in(key, 11)
    extra = 2 * REACH - 2
    rows_here = jnp.arange(NBR, dtype=jnp.int32)
    fixed = jnp.stack([jnp.zeros((NBR,), jnp.int32), jnp.full((NBR,), REACH, jnp.int32), jnp.full((NBR,), -REACH, jnp.int32)], axis=1)
    if KMAX > 3:
        near = jnp.concatenate([jnp.arange(-REACH + 1, 0, dtype=jnp.int32), jnp.arange(1, REACH, dtype=jnp.int32)])
        scores = jax.random.randint(key, (NBR, extra), 0, 1 << 20) * extra + jnp.arange(extra, dtype=jnp.int32)[None, :]
        order = jnp.argsort(scores, axis=1)
        others = near[order][:, :KMAX - 3]
        offsets = jnp.concatenate([fixed, others], axis=1)
    else:
        offsets = fixed[:, :KMAX]
    return jnp.mod(rows_here[:, None] + offsets, NBR).astype(jnp.int32)


def draw_block_counts(key, part):
    key = jax.random.fold_in(key, 23)
    first_key, second_key = jax.random.split(key)
    counts = jax.random.randint(first_key, (NBR,), 3, KMAX + 1)
    dense = jax.random.randint(second_key, (NBR // BR_DEV,), 0, 3) == 0
    counts = jnp.where(jnp.repeat(dense, BR_DEV), KMAX, counts)
    return counts.at[0].set(KMAX).astype(jnp.int32)


def shard_levels(stream_key, dims, cuts, least, high):
    level = 1.0
    for dim, shards_of in cuts:
        draws = jax.random.uniform(jax.random.fold_in(jax.random.fold_in(stream_key, 6), dim), (shards_of,), jnp.float32, least / len(cuts), high / len(cuts))
        level = level * jnp.repeat(jnp.exp(draws), dims[dim] // shards_of).reshape((-1,) + (1,) * (len(dims) - 1 - dim))
    return level


def bell_draw(key, extent, scale, limit, pieces=(), held_as=jnp.bfloat16):
    drawn = scale * jax.random.normal(key, extent, jnp.float32)
    if pieces:
        drawn = drawn * shard_levels(key, extent, pieces, -0.22, 0.18)
    return jnp.clip(drawn, -limit, limit).astype(held_as)


def setup_inputs(seed: int = 0) -> dict:
    arg_keys = jax.random.split(jax.random.key(seed), 6)
    return {
        "vectors": bell_draw(arg_keys[0], (VCOLS, NROWS), 1.0, 6.0, ((0, 8), (1, 32)), jnp.float32),
        "onsite": jnp.clip(jax.random.uniform(arg_keys[1], (NROWS,), jnp.float32, -2.0, 2.0) * shard_levels(arg_keys[1], (NROWS,), ((0, 32),), -0.4, 0.0), -2.0, 2.0),
        "h_blocks": bell_draw(arg_keys[2], (NBR, KMAX, BLOCK, BLOCK), (BLOCK * KMAX) ** -0.5, 0.1875, ((0, 32),), jnp.float32),
        "block_cols": draw_block_cols(jax.random.fold_in(arg_keys[5], 71), 0),
        "block_counts": draw_block_counts(jax.random.fold_in(arg_keys[5], 71), 0),
    }


filter_center = 1.0
filter_half = 2.0


def apply_hamiltonian(field, onsite, h_blocks, block_cols, block_counts):
    vcount = field.shape[0]
    nblocks = block_cols.shape[0]
    field3 = field.reshape(vcount, nblocks, BLOCK)
    slot_ids = jnp.arange(KMAX, dtype=jnp.int32)

    def one_row(items):
        blocks, columns, count = items
        weight = (slot_ids < count).astype(jnp.float32)
        picked = field3[:, columns, :] * weight[None, :, None]
        return jnp.einsum("vkj,kij->vi", picked, blocks, precision=lax.Precision.HIGHEST)

    strips = lax.map(one_row, (h_blocks, block_cols, block_counts))
    return jnp.transpose(strips, (1, 0, 2)).reshape(vcount, nblocks * BLOCK) + onsite[None, :] * field


def reference(vectors, onsite, h_blocks, block_cols, block_counts):
    first = (apply_hamiltonian(vectors, onsite, h_blocks, block_cols, block_counts) - filter_center * vectors) / filter_half
    second = apply_hamiltonian(first, onsite, h_blocks, block_cols, block_counts) - filter_center * first
    filtered = 2.0 * second / filter_half - vectors
    correlation = jnp.dot(filtered, filtered.T, precision=lax.Precision.HIGHEST, preferred_element_type=jnp.float32) / filtered.shape[1]
    return filtered, correlation
```

```python
import functools

import jax
import jax.numpy as jnp
from jax import lax
from jax.experimental import pallas as pl
from jax.experimental.pallas import tpu as pltpu
from jax.sharding import PartitionSpec as P

REACH = 4
BLOCK = 128

filter_center = 1.0
filter_half = 2.0

f32, bf16 = jnp.float32, jnp.bfloat16
VMEM = pl.BlockSpec(memory_space=pltpu.VMEM)
SMEM = pl.BlockSpec(memory_space=pltpu.SMEM)
ANY = pl.BlockSpec(memory_space=pl.ANY)


def halves(x):
    high = x.astype(bf16)
    return high, (x - high.astype(f32)).astype(bf16)


def load_blocks(table, pieces):
    vcount = table.shape[1] // 2
    for ref, start, blocks in pieces:
        for b in range(blocks):
            high, low = halves(ref[:, b * BLOCK : (b + 1) * BLOCK])
            table[start + b, 0:vcount] = high
            table[start + b, vcount : 2 * vcount] = low
    table[table.shape[0] - 1] = jnp.zeros(table.shape[1:], bf16)


def apply_rows(count, unroll, row_of, cols, counts, nblocks, table, h_hbm, h_buf, sems, finish):
    slots = h_buf.shape[1]
    empty = table.shape[0] - 1

    def fetch(i):
        return pltpu.make_async_copy(h_hbm.at[row_of(i)], h_buf.at[i], sems.at[i])

    def product(i):
        row = row_of(i)
        here = cols[row, 0]
        used = counts[row]
        picked = []
        for k in range(slots):
            shift = lax.rem(cols[row, k] - here + (REACH + nblocks), nblocks)
            picked.append(table[jnp.where(k < used, row + shift, empty)])
        left = jnp.concatenate(picked, axis=1)
        split = [halves(h_buf[i, k]) for k in range(slots)]
        right = jnp.concatenate(
            [
                jnp.concatenate([high for high, _ in split], axis=1),
                jnp.concatenate([low for _, low in split], axis=1),
            ],
            axis=0,
        )
        both = lax.dot_general(left, right, (((1,), (1,)), ((), ())), preferred_element_type=f32)
        v = left.shape[0] // 2
        return (both[:v, :BLOCK] + both[:v, BLOCK:]) + (both[v:, :BLOCK] + both[v:, BLOCK:])

    def step(s, carry):
        for u in range(unroll):
            fetch(s * unroll + u).wait()
        for u in range(unroll):
            i = s * unroll + u
            finish(i, row_of(i), product(i))
        return carry

    return fetch, lambda: lax.fori_loop(0, count // unroll, step, 0)


def columns(ref, block, count=1):
    return ref[:, pl.ds(pl.multiple_of(block * BLOCK, BLOCK), count * BLOCK)]


def set_columns(ref, block, value):
    ref[:, pl.ds(pl.multiple_of(block * BLOCK, BLOCK), BLOCK)] = value


def run_all(count, fetch):
    def one(i, carry):
        fetch(i).start()
        return carry

    lax.fori_loop(0, count, one, 0)


def first_inner(nblocks, local, cols, counts, onsite, field, h_hbm, out, table, h_buf, sems):
    count = local - 2 * REACH

    def row_of(i):
        return i + REACH

    def finish(i, row, total):
        diag = onsite[pl.ds(row, 1), :] - filter_center
        set_columns(out, i, (total + diag * columns(field, row)) / filter_half)

    fetch, loop = apply_rows(
        count, 4, row_of, cols, counts, nblocks, table, h_hbm, h_buf, sems, finish
    )
    run_all(count, fetch)
    load_blocks(table, [(field, REACH, local)])
    loop()


def first_edge(
    nblocks, local, cols, counts, onsite, before, field, after, h_hbm, low, high, table, h_buf, sems
):
    count = 2 * REACH

    def row_of(i):
        return jnp.where(i < REACH, i, i + local - 2 * REACH)

    def finish(i, row, total):
        diag = onsite[pl.ds(row, 1), :] - filter_center
        value = (total + diag * columns(field, row)) / filter_half

        @pl.when(i < REACH)
        def _():
            set_columns(low, i, value)

        @pl.when(i >= REACH)
        def _():
            set_columns(high, i - REACH, value)

    fetch, loop = apply_rows(
        count, 4, row_of, cols, counts, nblocks, table, h_hbm, h_buf, sems, finish
    )
    run_all(count, fetch)
    pieces = [(before, 0, REACH), (after, local + REACH, REACH)]
    pieces.append((field.at[:, 0 : 2 * REACH * BLOCK], REACH, 2 * REACH))
    pieces.append((field.at[:, (local - 2 * REACH) * BLOCK :], local - REACH, 2 * REACH))
    load_blocks(table, pieces)
    loop()


def second_inner(
    nblocks, local, groups, where, cols, counts, onsite, inner, field, h_hbm, out, parts, table, h_buf, sems
):
    count = local - 4 * REACH
    each = count // groups

    def row_of(i):
        k = i // each
        return lax.rem(where[0] + k, groups) * each + (i - k * each) + 2 * REACH

    def finish(i, row, total):
        diag = onsite[pl.ds(row, 1), :] - filter_center
        second = total + diag * columns(inner, row - REACH)
        value = 2.0 * second / filter_half - columns(field, row)
        set_columns(out, row - 2 * REACH, value)
        k = i // each
        parts[k, :, pl.ds(pl.multiple_of((i - k * each) * BLOCK, BLOCK), BLOCK)] = value

    fetch, loop = apply_rows(
        count, 4, row_of, cols, counts, nblocks, table, h_hbm, h_buf, sems, finish
    )
    run_all(count, fetch)
    load_blocks(table, [(inner, 2 * REACH, local - 2 * REACH)])
    loop()


def second_edge(
    nblocks, local, groups, where, cols, counts, onsite, before, low, inner, high, after, field, h_hbm,
    out_low, out_high, parts, table, h_buf, sems, middle,
):
    half = 2 * REACH
    count = 2 * half
    each = count // groups

    def place_of(i):
        k = i // each
        return lax.rem(where[0] + k, groups) * each + (i - k * each)

    def row_of(i):
        m = place_of(i)
        return jnp.where(m < half, m, m + local - 2 * half)

    def finish(i, row, total):
        diag = onsite[pl.ds(row, 1), :] - filter_center
        m = place_of(i)
        second = total + diag * columns(middle, m)
        value = 2.0 * second / filter_half - columns(field, row)

        @pl.when(m < half)
        def _():
            set_columns(out_low, m, value)

        @pl.when(m >= half)
        def _():
            set_columns(out_high, m - half, value)

        k = i // each
        parts[k, :, pl.ds(pl.multiple_of((i - k * each) * BLOCK, BLOCK), BLOCK)] = value

    fetch, loop = apply_rows(
        count, 4, row_of, cols, counts, nblocks, table, h_hbm, h_buf, sems, finish
    )
    run_all(count, fetch)
    reach = REACH * BLOCK
    middle[:, 0:reach] = low[...]
    middle[:, reach : 2 * reach] = inner[:, 0:reach]
    middle[:, 2 * reach : 3 * reach] = inner[:, inner.shape[1] - reach :]
    middle[:, 3 * reach :] = high[...]
    load_blocks(
        table,
        [
            (before, 0, REACH),
            (low, REACH, REACH),
            (inner.at[:, 0 : 2 * reach], 2 * REACH, 2 * REACH),
            (inner.at[:, inner.shape[1] - 2 * reach :], local - 2 * REACH, 2 * REACH),
            (high, local, REACH),
            (after, local + REACH, REACH),
        ],
    )
    loop()


def gram(groups, scale, where, *refs):
    sent, out = refs[: 2 * groups], refs[2 * groups]
    high, low, both = refs[2 * groups + 1 :]
    vcount, width = sent[0].shape[-2:]
    for k in range(groups):
        place = pl.multiple_of(lax.rem(where[0] + (groups - k), groups) * vcount, vcount)
        for c in range(2):
            ref = sent[2 * k + c]
            block = ref[0] if k == 0 else ref[...]
            a, b = halves(block)
            high[pl.ds(place, vcount), c * width : (c + 1) * width] = a
            low[pl.ds(place, vcount), c * width : (c + 1) * width] = b
    nt = (((1,), (1,)), ((), ()))
    a, b = high[...], low[...]
    both[...] = (
        lax.dot_general(a, a, nt, preferred_element_type=f32)
        + lax.dot_general(a, b, nt, preferred_element_type=f32)
        + lax.dot_general(b, a, nt, preferred_element_type=f32)
    ) * scale
    for k in range(groups):
        place = pl.multiple_of(lax.rem(where[0] + (groups - k), groups) * vcount, vcount)
        out[k] = both[pl.ds(place, vcount), :]


def params():
    return pltpu.CompilerParams(vmem_limit_bytes=40 * 1024 * 1024)


def cost(rows, slots, vcount):
    return pl.CostEstimate(
        flops=rows * slots * BLOCK * BLOCK * vcount * 2 * 6,
        bytes_accessed=rows * slots * BLOCK * BLOCK * 4,
        transcendentals=0,
    )


def on_device(vectors, onsite, h_blocks, block_cols, block_counts):
    vcount, width = vectors.shape
    local, slots = block_cols.shape
    ranks = lax.axis_size("rows")
    groups = lax.axis_size("cols")
    nblocks = local * ranks
    reach = REACH * BLOCK
    where = lax.axis_index("cols").astype(jnp.int32).reshape(1)
    onsite2 = onsite.reshape(local, BLOCK)

    def shape(*dims):
        return jax.ShapeDtypeStruct(dims, f32)

    def scratch(rows):
        return [
            pltpu.VMEM((local + 2 * REACH + 1, 2 * vcount, BLOCK), bf16),
            pltpu.VMEM((rows, slots, BLOCK, BLOCK), f32),
            pltpu.SemaphoreType.DMA((rows,)),
        ]

    up = [(i, (i + 1) % ranks) for i in range(ranks)]
    down = [(j, i) for i, j in up]

    def around(low, high):
        return lax.ppermute(high, "rows", up), lax.ppermute(low, "rows", down)

    before, after = around(vectors[:, :reach], vectors[:, width - reach :])

    n = local - 2 * REACH
    inner = pl.pallas_call(
        functools.partial(first_inner, nblocks, local),
        in_specs=[SMEM, SMEM, VMEM, VMEM, ANY],
        out_specs=VMEM,
        out_shape=shape(vcount, n * BLOCK),
        scratch_shapes=scratch(n),
        compiler_params=params(),
        cost_estimate=cost(n, slots, vcount),
        name="first_inner",
    )(block_cols, block_counts, onsite2, vectors, h_blocks)

    n = 2 * REACH
    low, high = pl.pallas_call(
        functools.partial(first_edge, nblocks, local),
        in_specs=[SMEM, SMEM, VMEM, VMEM, VMEM, VMEM, ANY],
        out_specs=(VMEM, VMEM),
        out_shape=(shape(vcount, reach), shape(vcount, reach)),
        scratch_shapes=scratch(n),
        compiler_params=params(),
        cost_estimate=cost(n, slots, vcount),
        name="first_edge",
    )(block_cols, block_counts, onsite2, before, vectors, after, h_blocks)

    before, after = around(low, high)

    n = local - 4 * REACH
    out_inner, parts_inner = pl.pallas_call(
        functools.partial(second_inner, nblocks, local, groups),
        in_specs=[SMEM, SMEM, SMEM, VMEM, VMEM, VMEM, ANY],
        out_specs=(VMEM, VMEM),
        out_shape=(shape(vcount, n * BLOCK), shape(groups, vcount, n * BLOCK // groups)),
        scratch_shapes=scratch(n),
        compiler_params=params(),
        cost_estimate=cost(n, slots, vcount),
        name="second_inner",
    )(where, block_cols, block_counts, onsite2, inner, vectors, h_blocks)

    n = 4 * REACH
    out_low, out_high, parts_edge = pl.pallas_call(
        functools.partial(second_edge, nblocks, local, groups),
        in_specs=[SMEM, SMEM, SMEM, VMEM, VMEM, VMEM, VMEM, VMEM, VMEM, VMEM, ANY],
        out_specs=(VMEM, VMEM, VMEM),
        out_shape=(
            shape(vcount, 2 * reach),
            shape(vcount, 2 * reach),
            shape(groups, vcount, n * BLOCK // groups),
        ),
        scratch_shapes=scratch(n) + [pltpu.VMEM((vcount, n * BLOCK), f32)],
        compiler_params=params(),
        cost_estimate=cost(n, slots, vcount),
        name="second_edge",
    )(where, block_cols, block_counts, onsite2, before, low, inner, high, after, vectors, h_blocks)

    filtered = jnp.concatenate([out_low, out_inner, out_high], axis=1)

    def turn(x, k):
        return lax.ppermute(x, "cols", [(i, (i + k) % groups) for i in range(groups)])

    order = sorted(range(1, groups), key=lambda k: -min(k, groups - k))
    got = {0: (parts_inner, parts_edge)}
    first_got = {k: turn(parts_inner[k], k) for k in order}
    second_got = {k: turn(parts_edge[k], k) for k in order}
    for k in order:
        got[k] = (first_got[k], second_got[k])
    flat = [x for k in range(groups) for x in got[k]]
    total_v = vcount * groups
    total_w = width // groups
    terms = pl.pallas_call(
        functools.partial(gram, groups, 1.0 / (width * ranks)),
        in_specs=[SMEM] + [VMEM] * (2 * groups),
        out_specs=VMEM,
        out_shape=shape(groups, vcount, total_v),
        scratch_shapes=[
            pltpu.VMEM((total_v, total_w), bf16),
            pltpu.VMEM((total_v, total_w), bf16),
            pltpu.VMEM((total_v, total_v), f32),
        ],
        compiler_params=params(),
        name="gram",
    )(where, *flat)

    mine = terms[0]
    for x in [turn(terms[k], -k) for k in order]:
        mine = mine + x

    step = 1
    while step < ranks:
        mine = mine + lax.ppermute(mine, "rows", [(i, i ^ step) for i in range(ranks)])
        step *= 2
    return (filtered, mine)


def solution(mesh):
    return jax.shard_map(
        on_device,
        mesh=mesh,
        in_specs=(
            P("cols", "rows"),
            P("rows"),
            P("rows", None, None, None),
            P("rows", None),
            P("rows"),
        ),
        out_specs=(P("cols", "rows"), P("cols", None)),
        check_vma=False,
    )
```

```python
import functools

import jax
import jax.numpy as jnp
from jax import lax
from jax.experimental import pallas as pl
from jax.experimental.pallas import tpu as pltpu
from jax.sharding import PartitionSpec as P

REACH = 4
BLOCK = 128

filter_center = 1.0
filter_half = 2.0

f32, bf16 = jnp.float32, jnp.bfloat16
VMEM = pl.BlockSpec(memory_space=pltpu.VMEM)
SMEM = pl.BlockSpec(memory_space=pltpu.SMEM)
HBM = pl.BlockSpec(memory_space=pltpu.HBM)
NT = (((1,), (1,)), ((), ()))


def halves(x):
    high = x.astype(bf16)
    return high, (x - high.astype(f32)).astype(bf16)


def load_blocks(table, pieces):
    vcount = table.shape[1] // 2
    for ref, block, slot, blocks in pieces:
        for b in range(blocks):
            high, low = halves(ref[:, (block + b) * BLOCK : (block + b + 1) * BLOCK])
            table[slot + b, 0:vcount] = high
            table[slot + b, vcount : 2 * vcount] = low
    table[table.shape[0] - 1] = jnp.zeros(table.shape[1:], bf16)


def columns(ref, block):
    return ref[:, pl.ds(pl.multiple_of(block * BLOCK, BLOCK), BLOCK)]


def set_columns(ref, block, value):
    ref[:, pl.ds(pl.multiple_of(block * BLOCK, BLOCK), BLOCK)] = value


def row_product(row, nblocks, cols, counts, table, h):
    slots = h.shape[1]
    here = cols[0, row]
    used = counts[row]
    picked = []
    for k in range(slots):
        shift = cols[k, row] - here
        shift = jnp.where(shift > REACH, shift - nblocks, shift)
        shift = jnp.where(shift < -REACH, shift + nblocks, shift)
        picked.append(table[jnp.where(k < used, row + shift + REACH, table.shape[0] - 1)])
    left = jnp.concatenate(picked, axis=1)
    split = [halves(h[row, k]) for k in range(slots)]
    right = jnp.concatenate(
        [
            jnp.concatenate([high for high, _ in split], axis=1),
            jnp.concatenate([low for _, low in split], axis=1),
        ],
        axis=0,
    )
    both = lax.dot_general(left, right, NT, preferred_element_type=f32)
    v = left.shape[0] // 2
    return (both[:v, :BLOCK] + both[:v, BLOCK:]) + (both[v:, :BLOCK] + both[v:, BLOCK:])


def first_value(row, total, onsite, field):
    diag = onsite[pl.ds(row, 1), :] - filter_center
    return (total + diag * columns(field, row)) / filter_half


def first_inner(
    nblocks, local, cols_hbm, counts_hbm, onsite_hbm, field_hbm, h_hbm,
    cols, counts, h, field, onsite, out, table, sems, small,
):
    count = local - 2 * REACH
    unroll = 4

    def fetch(row):
        return pltpu.make_async_copy(h_hbm.at[row], h.at[row], sems.at[row])

    copies = [
        pltpu.make_async_copy(a, b, small.at[n])
        for n, (a, b) in enumerate(
            [(field_hbm, field), (cols_hbm, cols), (counts_hbm, counts), (onsite_hbm, onsite)]
        )
    ]
    for copy in copies:
        copy.start()

    def begin(i, carry):
        fetch(lax.rem(i + REACH, local)).start()
        return carry

    lax.fori_loop(0, local, begin, 0)
    for copy in copies:
        copy.wait()
    load_blocks(table, [(field, 0, REACH, local)])

    def step(s, carry):
        for u in range(unroll):
            fetch(s * unroll + u + REACH).wait()
        for u in range(unroll):
            i = s * unroll + u
            row = i + REACH
            total = row_product(row, nblocks, cols, counts, table, h)
            set_columns(out, i, first_value(row, total, onsite, field))
        return carry

    lax.fori_loop(0, count // unroll, step, 0)

    def rest(i, carry):
        fetch(lax.rem(i + local - REACH, local)).wait()
        return carry

    lax.fori_loop(0, 2 * REACH, rest, 0)


def first_edge(nblocks, local, cols, counts, onsite, before, field, after, h, out, table):
    load_blocks(
        table,
        [
            (before, 0, 0, REACH),
            (field, 0, REACH, 2 * REACH),
            (field, local - 2 * REACH, local - REACH, 2 * REACH),
            (after, 0, local + REACH, REACH),
        ],
    )
    unroll = 4

    def step(s, carry):
        for u in range(unroll):
            i = s * unroll + u
            row = jnp.where(i < REACH, i, i + local - 2 * REACH)
            total = row_product(row, nblocks, cols, counts, table, h)
            set_columns(out, i, first_value(row, total, onsite, field))
        return carry

    lax.fori_loop(0, 2 * REACH // unroll, step, 0)


def second_value(row, total, onsite, first, field):
    diag = onsite[pl.ds(row, 1), :] - filter_center
    return 2.0 * (total + diag * first) / filter_half - columns(field, row)


def second_inner(nblocks, local, cols, counts, onsite, edge, inner, field, h, out, table):
    load_blocks(
        table,
        [
            (edge, 0, REACH, REACH),
            (inner, 0, 2 * REACH, local - 2 * REACH),
            (edge, REACH, local, REACH),
        ],
    )
    unroll = 4

    def step(s, carry):
        for u in range(unroll):
            i = s * unroll + u
            row = i + REACH
            total = row_product(row, nblocks, cols, counts, table, h)
            set_columns(out, i, second_value(row, total, onsite, columns(inner, i), field))
        return carry

    lax.fori_loop(0, (local - 2 * REACH) // unroll, step, 0)


def second_edge(
    nblocks, local, groups, cols, counts, onsite, before, edge, inner, after, field, done, h,
    out, parts, table,
):
    load_blocks(
        table,
        [
            (before, 0, 0, REACH),
            (edge, 0, REACH, REACH),
            (inner, 0, 2 * REACH, REACH),
            (inner, local - 3 * REACH, local - REACH, REACH),
            (edge, REACH, local, REACH),
            (after, 0, local + REACH, REACH),
        ],
    )
    out[:, REACH * BLOCK : (local - REACH) * BLOCK] = done[...]
    unroll = 4

    def step(s, carry):
        for u in range(unroll):
            i = s * unroll + u
            row = jnp.where(i < REACH, i, i + local - 2 * REACH)
            total = row_product(row, nblocks, cols, counts, table, h)
            set_columns(out, row, second_value(row, total, onsite, columns(edge, i), field))
        return carry

    lax.fori_loop(0, 2 * REACH // unroll, step, 0)
    where = lax.axis_index("cols")
    width = parts.shape[2]
    for k in range(groups):
        place = lax.rem(where + k, groups) * width
        parts[k] = out[:, pl.ds(pl.multiple_of(place, width), width)]


def gram(groups, scale, own, *refs):
    got = refs[: groups - 1]
    keep, give, high, low, both = refs[groups - 1 :]
    vcount = own.shape[1]
    where = lax.axis_index("cols")
    core = lax.rem(lax.axis_index("rows"), 2)

    def place(k):
        return pl.multiple_of(lax.rem(where + k, groups) * vcount, vcount)

    for k in range(groups):
        a, b = halves(own[0] if k == 0 else got[k - 1][...])
        at = place(groups - k)
        high[pl.ds(at, vcount), :] = a
        low[pl.ds(at, vcount), :] = b
    a, b = high[...], low[...]
    both[...] = (
        lax.dot_general(a, a, NT, preferred_element_type=f32)
        + lax.dot_general(a, b, NT, preferred_element_type=f32)
        + lax.dot_general(b, a, NT, preferred_element_type=f32)
    ) * scale
    half = groups // 2
    for j in range(half):
        even, odd = (half, 0) if j == 0 else (j, groups - j)
        keep[j] = both[pl.ds(place(jnp.where(core == 0, even, odd)), vcount), :]
        give[j] = both[pl.ds(place(jnp.where(core == 0, odd, even)), vcount), :]


def params(mebibytes):
    return pltpu.CompilerParams(vmem_limit_bytes=mebibytes * 1024 * 1024)


def cost(rows, slots, vcount):
    return pl.CostEstimate(
        flops=rows * slots * BLOCK * BLOCK * vcount * 2 * 4,
        bytes_accessed=rows * slots * BLOCK * BLOCK * 4,
        transcendentals=0,
    )


def on_device(vectors, onsite, h_blocks, block_cols, block_counts):
    vcount, width = vectors.shape
    local, slots = block_cols.shape
    ranks = lax.axis_size("rows")
    groups = lax.axis_size("cols")
    nblocks = local * ranks
    reach = REACH * BLOCK
    edge_rows, inner_rows = 2 * REACH, local - 2 * REACH
    cols = block_cols.T
    onsite = onsite.reshape(local, BLOCK)

    def shape(*dims):
        return jax.ShapeDtypeStruct(dims, f32)

    table = pltpu.VMEM((local + 2 * REACH + 1, 2 * vcount, BLOCK), bf16)
    up = [(i, (i + 1) % ranks) for i in range(ranks)]
    down = [(j, i) for i, j in up]

    def around(low, high):
        return lax.ppermute(high, "rows", up), lax.ppermute(low, "rows", down)

    before, after = around(vectors[:, :reach], vectors[:, width - reach :])

    cols, counts, h, field, onsite, inner = pl.pallas_call(
        functools.partial(first_inner, nblocks, local),
        in_specs=[HBM] * 5,
        out_specs=(SMEM,) * 2 + (VMEM,) * 4,
        out_shape=(
            pltpu.SMEM(cols.shape, jnp.int32),
            pltpu.SMEM(block_counts.shape, jnp.int32),
            pltpu.VMEM(h_blocks.shape, f32),
            pltpu.VMEM(vectors.shape, f32),
            pltpu.VMEM(onsite.shape, f32),
            pltpu.VMEM((vcount, inner_rows * BLOCK), f32),
        ),
        scratch_shapes=[
            table,
            pltpu.SemaphoreType.DMA((local,)),
            pltpu.SemaphoreType.DMA((4,)),
        ],
        compiler_params=params(8),
        cost_estimate=cost(local, slots, vcount),
        name="first_inner",
    )(*[pltpu.with_memory_space_constraint(x, pltpu.HBM) for x in (cols, block_counts, onsite, vectors, h_blocks)])

    edge = pl.pallas_call(
        functools.partial(first_edge, nblocks, local),
        in_specs=[SMEM, SMEM] + [VMEM] * 5,
        out_specs=VMEM,
        out_shape=shape(vcount, edge_rows * BLOCK),
        scratch_shapes=[table],
        compiler_params=params(8),
        cost_estimate=cost(edge_rows, slots, vcount),
        name="first_edge",
    )(cols, counts, onsite, before, field, after, h)

    before, after = around(edge[:, :reach], edge[:, reach:])

    done = pl.pallas_call(
        functools.partial(second_inner, nblocks, local),
        in_specs=[SMEM, SMEM] + [VMEM] * 5,
        out_specs=VMEM,
        out_shape=shape(vcount, inner_rows * BLOCK),
        scratch_shapes=[table],
        compiler_params=params(8),
        cost_estimate=cost(inner_rows, slots, vcount),
        name="second_inner",
    )(cols, counts, onsite, edge, inner, field, h)

    filtered, parts = pl.pallas_call(
        functools.partial(second_edge, nblocks, local, groups),
        in_specs=[SMEM, SMEM] + [VMEM] * 8,
        out_specs=(VMEM, VMEM),
        out_shape=(shape(vcount, width), shape(groups, vcount, width // groups)),
        scratch_shapes=[table],
        compiler_params=params(8),
        cost_estimate=cost(edge_rows, slots, vcount),
        name="second_edge",
    )(cols, counts, onsite, before, edge, inner, after, field, done, h)

    order = sorted(range(1, groups), key=lambda k: -min(k, groups - k))
    got = {}
    for k in order:
        pairs = [(i, (i + k) % groups) for i in range(groups)]
        got[k] = lax.ppermute(parts[k], "cols", pairs)
    total = vcount * groups
    half = groups // 2
    keep, give = pl.pallas_call(
        functools.partial(gram, groups, 1.0 / (width * ranks)),
        in_specs=[VMEM] * groups,
        out_specs=(VMEM, VMEM),
        out_shape=(shape(half, vcount, total), shape(half, vcount, total)),
        scratch_shapes=[
            pltpu.VMEM((total, width // groups), bf16),
            pltpu.VMEM((total, width // groups), bf16),
            pltpu.VMEM((total, total), f32),
        ],
        compiler_params=params(8),
        name="gram",
    )(parts, *[got[k] for k in range(1, groups)])

    keep = keep + lax.ppermute(give, "rows", [(i, i ^ 1) for i in range(ranks)])
    terms = []
    for j in range(half):
        pairs = []
        for r in range(ranks):
            shift = (half if j == 0 else j) if r % 2 == 0 else -j
            pairs += [(r * groups + z, r * groups + (z + shift) % groups) for z in range(groups)]
        terms.append(lax.ppermute(keep[j], ("rows", "cols"), pairs))
    mine = sum(terms[1:], terms[0])

    side = 4
    for stride in (2, 2 * side):
        terms = []
        for k in range(1, side):
            pairs = []
            for r in range(ranks):
                at = r // stride % side
                pairs.append((r, r + ((at + k) % side - at) * stride))
            terms.append(lax.ppermute(mine, "rows", pairs))
        mine = sum(terms, mine)
    mine = mine + lax.ppermute(mine, "rows", [(i, i ^ 1) for i in range(ranks)])
    return (filtered, mine)


def solution(mesh):
    return jax.shard_map(
        on_device,
        mesh=mesh,
        in_specs=(
            P("cols", "rows"),
            P("rows"),
            P("rows", None, None, None),
            P("rows", None),
            P("rows"),
        ),
        out_specs=(P("cols", "rows"), P("cols", None)),
        check_vma=False,
    )
```

```python
import functools

import jax
import jax.numpy as jnp
from jax import lax
from jax.experimental import pallas as pl
from jax.experimental.pallas import tpu as pltpu
from jax.sharding import PartitionSpec as P

REACH = 4
BLOCK = 128

filter_center = 1.0
filter_half = 2.0

f32, bf16 = jnp.float32, jnp.bfloat16
VMEM = pl.BlockSpec(memory_space=pltpu.VMEM)
SMEM = pl.BlockSpec(memory_space=pltpu.SMEM)
HBM = pl.BlockSpec(memory_space=pltpu.HBM)
NT = (((1,), (1,)), ((), ()))


def halves(x):
    high = x.astype(bf16)
    return high, (x - high.astype(f32)).astype(bf16)


def load_blocks(table, pieces):
    vcount = table.shape[1] // 2
    for ref, block, slot, blocks in pieces:
        for b in range(blocks):
            high, low = halves(ref[:, (block + b) * BLOCK : (block + b + 1) * BLOCK])
            table[slot + b, 0:vcount] = high
            table[slot + b, vcount : 2 * vcount] = low
    table[table.shape[0] - 1] = jnp.zeros(table.shape[1:], bf16)


def is_first_core():
    return lax.rem(lax.axis_index("rows"), 2) == 0


def outer_slots(local):
    first = is_first_core()
    return jnp.where(first, local + REACH, 0), jnp.where(first, 0, local + REACH)


def split_ends(ref, near, far, count):
    width = count * BLOCK
    first = is_first_core()
    high = ref.shape[1] - width
    near[...] = ref[:, pl.ds(pl.multiple_of(jnp.where(first, high, 0), BLOCK), width)]
    far[...] = ref[:, pl.ds(pl.multiple_of(jnp.where(first, 0, high), BLOCK), width)]


def columns(ref, block):
    return ref[:, pl.ds(pl.multiple_of(block * BLOCK, BLOCK), BLOCK)]


def set_columns(ref, block, value):
    ref[:, pl.ds(pl.multiple_of(block * BLOCK, BLOCK), BLOCK)] = value


def row_product(row, nblocks, cols, counts, table, h):
    slots = h.shape[1]
    here = cols[0, row]
    used = counts[row]
    picked = []
    for k in range(slots):
        shift = cols[k, row] - here
        shift = jnp.where(shift > REACH, shift - nblocks, shift)
        shift = jnp.where(shift < -REACH, shift + nblocks, shift)
        picked.append(table[jnp.where(k < used, row + shift + REACH, table.shape[0] - 1)])
    left = jnp.concatenate(picked, axis=1)
    split = [halves(h[row, k]) for k in range(slots)]
    right = jnp.concatenate(
        [
            jnp.concatenate([high for high, _ in split], axis=1),
            jnp.concatenate([low for _, low in split], axis=1),
        ],
        axis=0,
    )
    both = lax.dot_general(left, right, NT, preferred_element_type=f32)
    v = left.shape[0] // 2
    return (both[:v, :BLOCK] + both[:v, BLOCK:]) + (both[v:, :BLOCK] + both[v:, BLOCK:])


def first_value(row, total, onsite, field):
    diag = onsite[pl.ds(row, 1), :] - filter_center
    return (total + diag * columns(field, row)) / filter_half


def ends(field_hbm, near, far, sems):
    width = near.shape[1]
    high = field_hbm.shape[1] - width
    first = is_first_core()
    copies = []
    for n, (start, ref) in enumerate(
        [(jnp.where(first, 0, high), far), (jnp.where(first, high, 0), near)]
    ):
        part = field_hbm.at[:, pl.ds(pl.multiple_of(start, BLOCK), width)]
        copies.append(pltpu.make_async_copy(part, ref, sems.at[n]))
    for copy in copies:
        copy.start()
    for copy in copies:
        copy.wait()


def first_inner(
    nblocks, local, cols_hbm, counts_hbm, onsite_hbm, field_hbm, h_hbm,
    cols, counts, h, field, onsite, out, table, sems, small,
):
    count = local - 2 * REACH
    unroll = 4

    def fetch(row):
        return pltpu.make_async_copy(h_hbm.at[row], h.at[row], sems.at[row])

    copies = [
        pltpu.make_async_copy(a, b, small.at[n])
        for n, (a, b) in enumerate(
            [(field_hbm, field), (cols_hbm, cols), (counts_hbm, counts), (onsite_hbm, onsite)]
        )
    ]
    for copy in copies:
        copy.start()

    def begin(i, carry):
        fetch(lax.rem(i + REACH, local)).start()
        return carry

    lax.fori_loop(0, local, begin, 0)
    for copy in copies:
        copy.wait()
    load_blocks(table, [(field, 0, REACH, local)])

    def step(s, carry):
        for u in range(unroll):
            fetch(s * unroll + u + REACH).wait()
        for u in range(unroll):
            i = s * unroll + u
            row = i + REACH
            total = row_product(row, nblocks, cols, counts, table, h)
            set_columns(out, i, first_value(row, total, onsite, field))
        return carry

    lax.fori_loop(0, count // unroll, step, 0)

    def rest(i, carry):
        fetch(lax.rem(i + local - REACH, local)).wait()
        return carry

    lax.fori_loop(0, 2 * REACH, rest, 0)


def first_edge(
    nblocks, local, cols, counts, onsite, near, far, field, h, out, near_out, far_out, table
):
    near_slot, far_slot = outer_slots(local)
    load_blocks(
        table,
        [
            (near, 0, near_slot, REACH),
            (far, 0, far_slot, REACH),
            (field, 0, REACH, 2 * REACH),
            (field, local - 2 * REACH, local - REACH, 2 * REACH),
        ],
    )
    unroll = 4

    def step(s, carry):
        for u in range(unroll):
            i = s * unroll + u
            row = jnp.where(i < REACH, i, i + local - 2 * REACH)
            total = row_product(row, nblocks, cols, counts, table, h)
            set_columns(out, i, first_value(row, total, onsite, field))
        return carry

    lax.fori_loop(0, 2 * REACH // unroll, step, 0)
    split_ends(out, near_out, far_out, REACH)


def second_value(row, total, onsite, first, field):
    diag = onsite[pl.ds(row, 1), :] - filter_center
    return 2.0 * (total + diag * first) / filter_half - columns(field, row)


def second_inner(nblocks, local, cols, counts, onsite, edge, inner, field, h, out, table):
    load_blocks(
        table,
        [
            (edge, 0, REACH, REACH),
            (inner, 0, 2 * REACH, local - 2 * REACH),
            (edge, REACH, local, REACH),
        ],
    )
    unroll = 4

    def step(s, carry):
        for u in range(unroll):
            i = s * unroll + u
            row = i + REACH
            total = row_product(row, nblocks, cols, counts, table, h)
            set_columns(out, i, second_value(row, total, onsite, columns(inner, i), field))
        return carry

    lax.fori_loop(0, (local - 2 * REACH) // unroll, step, 0)


def second_edge(
    nblocks, local, cols, counts, onsite, near, far, edge, inner, field, done, h, out, parts, table
):
    near_slot, far_slot = outer_slots(local)
    load_blocks(
        table,
        [
            (near, 0, near_slot, REACH),
            (far, 0, far_slot, REACH),
            (edge, 0, REACH, REACH),
            (inner, 0, 2 * REACH, REACH),
            (inner, local - 3 * REACH, local - REACH, REACH),
            (edge, REACH, local, REACH),
        ],
    )
    out[:, REACH * BLOCK : (local - REACH) * BLOCK] = done[...]
    unroll = 4

    def step(s, carry):
        for u in range(unroll):
            i = s * unroll + u
            row = jnp.where(i < REACH, i, i + local - 2 * REACH)
            total = row_product(row, nblocks, cols, counts, table, h)
            set_columns(out, row, second_value(row, total, onsite, columns(edge, i), field))
        return carry

    lax.fori_loop(0, 2 * REACH // unroll, step, 0)
    width = parts.shape[2]
    for k in range(parts.shape[0]):
        parts[k] = out[:, k * width : (k + 1) * width]


def gram(scale, parts, keep, give):
    groups, vcount, width = parts.shape
    total = groups * vcount
    a, b = halves(parts[...].reshape(total, width))
    both = (
        lax.dot_general(a, a, NT, preferred_element_type=f32)
        + lax.dot_general(a, b, NT, preferred_element_type=f32)
        + lax.dot_general(b, a, NT, preferred_element_type=f32)
    ) * scale
    low = both[:, : total // 2].reshape(groups, vcount, total // 2)
    high = both[:, total // 2 :].reshape(groups, vcount, total // 2)
    first = is_first_core()
    keep[...] = jnp.where(first, low, high)
    give[...] = jnp.where(first, high, low)


def join(mine, other, out):
    first = is_first_core()
    half = mine.shape[1]
    out[:, :half] = jnp.where(first, mine[...], other[...])
    out[:, half:] = jnp.where(first, other[...], mine[...])


def params(mebibytes):
    return pltpu.CompilerParams(vmem_limit_bytes=mebibytes * 1024 * 1024)


def cost(rows, slots, vcount):
    return pl.CostEstimate(
        flops=rows * slots * BLOCK * BLOCK * vcount * 2 * 4,
        bytes_accessed=rows * slots * BLOCK * BLOCK * 4,
        transcendentals=0,
    )


def on_device(vectors, onsite, h_blocks, block_cols, block_counts):
    vcount, width = vectors.shape
    local, slots = block_cols.shape
    ranks = lax.axis_size("rows")
    groups = lax.axis_size("cols")
    nblocks = local * ranks
    reach = REACH * BLOCK
    edge_rows, inner_rows = 2 * REACH, local - 2 * REACH
    cols = block_cols.T
    onsite = onsite.reshape(local, BLOCK)

    def shape(*dims):
        return jax.ShapeDtypeStruct(dims, f32)

    table = pltpu.VMEM((local + 2 * REACH + 1, 2 * vcount, BLOCK), bf16)
    mate = [(i, i ^ 1) for i in range(ranks)]
    beyond = [(i, (i + 1 if i % 2 else i - 1) % ranks) for i in range(ranks)]

    def around(near, far):
        far = lax.ppermute(far, "rows", beyond)
        return lax.ppermute(near, "rows", mate), far

    def in_hbm(*arrays):
        return [pltpu.with_memory_space_constraint(x, pltpu.HBM) for x in arrays]

    near, far = pl.pallas_call(
        ends,
        in_specs=[HBM],
        out_specs=(VMEM, VMEM),
        out_shape=(pltpu.VMEM((vcount, reach), f32), pltpu.VMEM((vcount, reach), f32)),
        scratch_shapes=[pltpu.SemaphoreType.DMA((2,))],
        compiler_params=params(8),
        name="ends",
    )(*in_hbm(vectors))
    near, far = around(near, far)

    cols, counts, h, field, onsite, inner = pl.pallas_call(
        functools.partial(first_inner, nblocks, local),
        in_specs=[HBM] * 5,
        out_specs=(SMEM,) * 2 + (VMEM,) * 4,
        out_shape=(
            pltpu.SMEM(cols.shape, jnp.int32),
            pltpu.SMEM(block_counts.shape, jnp.int32),
            pltpu.VMEM(h_blocks.shape, f32),
            pltpu.VMEM(vectors.shape, f32),
            pltpu.VMEM(onsite.shape, f32),
            pltpu.VMEM((vcount, inner_rows * BLOCK), f32),
        ),
        scratch_shapes=[
            table,
            pltpu.SemaphoreType.DMA((local,)),
            pltpu.SemaphoreType.DMA((4,)),
        ],
        compiler_params=params(8),
        cost_estimate=cost(local, slots, vcount),
        name="first_inner",
    )(*in_hbm(cols, block_counts, onsite, vectors, h_blocks))

    edge, near, far = pl.pallas_call(
        functools.partial(first_edge, nblocks, local),
        in_specs=[SMEM, SMEM] + [VMEM] * 5,
        out_specs=(VMEM,) * 3,
        out_shape=(shape(vcount, 2 * reach), shape(vcount, reach), shape(vcount, reach)),
        scratch_shapes=[table],
        compiler_params=params(8),
        cost_estimate=cost(edge_rows, slots, vcount),
        name="first_edge",
    )(cols, counts, onsite, near, far, field, h)
    near, far = around(near, far)

    done = pl.pallas_call(
        functools.partial(second_inner, nblocks, local),
        in_specs=[SMEM, SMEM] + [VMEM] * 5,
        out_specs=VMEM,
        out_shape=shape(vcount, inner_rows * BLOCK),
        scratch_shapes=[table],
        compiler_params=params(8),
        cost_estimate=cost(inner_rows, slots, vcount),
        name="second_inner",
    )(cols, counts, onsite, edge, inner, field, h)

    filtered, parts = pl.pallas_call(
        functools.partial(second_edge, nblocks, local),
        in_specs=[SMEM, SMEM] + [VMEM] * 8,
        out_specs=(VMEM, VMEM),
        out_shape=(shape(vcount, width), shape(groups, vcount, width // groups)),
        scratch_shapes=[table],
        compiler_params=params(8),
        cost_estimate=cost(edge_rows, slots, vcount),
        name="second_edge",
    )(cols, counts, onsite, near, far, edge, inner, field, done, h)

    parts = lax.all_to_all(parts, "cols", 0, 0)
    total = vcount * groups
    keep, give = pl.pallas_call(
        functools.partial(gram, 1.0 / (width * ranks)),
        in_specs=[VMEM],
        out_specs=(VMEM, VMEM),
        out_shape=(shape(groups, vcount, total // 2), shape(groups, vcount, total // 2)),
        compiler_params=params(8),
        name="gram",
    )(parts)
    terms = lax.all_to_all(keep + lax.ppermute(give, "rows", mate), "cols", 0, 0)
    mine = jnp.sum(terms, axis=0)

    peers = ranks // 2
    same = [[2 * i + core for i in range(peers)] for core in range(2)]
    terms = jnp.broadcast_to(mine[None], (peers, *mine.shape))
    terms = lax.all_to_all(terms, "rows", 0, 0, axis_index_groups=same)
    mine = jnp.sum(terms, axis=0)
    other = lax.ppermute(mine, "rows", mate)
    correlation = pl.pallas_call(
        join,
        in_specs=[VMEM, VMEM],
        out_specs=VMEM,
        out_shape=shape(vcount, total),
        compiler_params=params(8),
        name="join",
    )(mine, other)
    return (filtered, correlation)


def solution(mesh):
    return jax.shard_map(
        on_device,
        mesh=mesh,
        in_specs=(
            P("cols", "rows"),
            P("rows"),
            P("rows", None, None, None),
            P("rows", None),
            P("rows"),
        ),
        out_specs=(P("cols", "rows"), P("cols", None)),
        check_vma=False,
    )
```

```python
import functools

import jax
import jax.numpy as jnp
from jax import lax
from jax.experimental import pallas as pl
from jax.experimental.pallas import tpu as pltpu
from jax.sharding import PartitionSpec as P

REACH = 4
BLOCK = 128

filter_center = 1.0
filter_half = 2.0

f32, bf16 = jnp.float32, jnp.bfloat16
VMEM = pl.BlockSpec(memory_space=pltpu.VMEM)
SMEM = pl.BlockSpec(memory_space=pltpu.SMEM)
HBM = pl.BlockSpec(memory_space=pltpu.HBM)
NT = (((1,), (1,)), ((), ()))


def halves(x):
    high = x.astype(bf16)
    return high, (x - high.astype(f32)).astype(bf16)


def load_blocks(table, pieces):
    vcount = table.shape[1] // 2
    for ref, block, slot, blocks in pieces:
        for b in range(blocks):
            high, low = halves(ref[:, (block + b) * BLOCK : (block + b + 1) * BLOCK])
            table[slot + b, 0:vcount] = high
            table[slot + b, vcount : 2 * vcount] = low
    table[table.shape[0] - 1] = jnp.zeros(table.shape[1:], bf16)


def is_first_core():
    return lax.rem(lax.axis_index("rows"), 2) == 0


def outer_slots(local):
    first = is_first_core()
    return jnp.where(first, local + REACH, 0), jnp.where(first, 0, local + REACH)


def split_ends(ref, near, far, count):
    width = count * BLOCK
    first = is_first_core()
    high = ref.shape[1] - width
    near[...] = ref[:, pl.ds(pl.multiple_of(jnp.where(first, high, 0), BLOCK), width)]
    far[...] = ref[:, pl.ds(pl.multiple_of(jnp.where(first, 0, high), BLOCK), width)]


def columns(ref, block):
    return ref[:, pl.ds(pl.multiple_of(block * BLOCK, BLOCK), BLOCK)]


def set_columns(ref, block, value):
    ref[:, pl.ds(pl.multiple_of(block * BLOCK, BLOCK), BLOCK)] = value


def row_product(row, nblocks, cols, counts, table, h):
    slots = h.shape[1]
    here = cols[0, row]
    used = counts[row]
    picked = []
    for k in range(slots):
        shift = cols[k, row] - here
        shift = jnp.where(shift > REACH, shift - nblocks, shift)
        shift = jnp.where(shift < -REACH, shift + nblocks, shift)
        picked.append(table[jnp.where(k < used, row + shift + REACH, table.shape[0] - 1)])
    left = jnp.concatenate(picked, axis=1)
    split = [halves(h[row, k]) for k in range(slots)]
    right = jnp.concatenate(
        [
            jnp.concatenate([high for high, _ in split], axis=1),
            jnp.concatenate([low for _, low in split], axis=1),
        ],
        axis=0,
    )
    both = lax.dot_general(left, right, NT, preferred_element_type=f32)
    v = left.shape[0] // 2
    return (both[:v, :BLOCK] + both[:v, BLOCK:]) + (both[v:, :BLOCK] + both[v:, BLOCK:])


def first_value(row, total, onsite, field):
    diag = onsite[pl.ds(row, 1), :] - filter_center
    return (total + diag * columns(field, row)) / filter_half


def ends(field_hbm, near, far, sems):
    width = near.shape[1]
    high = field_hbm.shape[1] - width
    first = is_first_core()
    copies = []
    for n, (start, ref) in enumerate(
        [(jnp.where(first, 0, high), far), (jnp.where(first, high, 0), near)]
    ):
        part = field_hbm.at[:, pl.ds(pl.multiple_of(start, BLOCK), width)]
        copies.append(pltpu.make_async_copy(part, ref, sems.at[n]))
    for copy in copies:
        copy.start()
    for copy in copies:
        copy.wait()


def first_inner(
    nblocks, local, cols_hbm, counts_hbm, onsite_hbm, field_hbm, h_hbm,
    cols, counts, h, field, onsite, out, table, sems, small,
):
    count = local - 2 * REACH
    unroll = 8

    def fetch(row):
        return pltpu.make_async_copy(h_hbm.at[row], h.at[row], sems.at[row])

    copies = [
        pltpu.make_async_copy(a, b, small.at[n])
        for n, (a, b) in enumerate(
            [(field_hbm, field), (cols_hbm, cols), (counts_hbm, counts), (onsite_hbm, onsite)]
        )
    ]
    for copy in copies:
        copy.start()

    def begin(i, carry):
        fetch(lax.rem(i + REACH, local)).start()
        return carry

    lax.fori_loop(0, local, begin, 0)
    for copy in copies:
        copy.wait()
    load_blocks(table, [(field, 0, REACH, local)])

    def step(s, carry):
        for u in range(unroll):
            fetch(s * unroll + u + REACH).wait()
        for u in range(unroll):
            i = s * unroll + u
            row = i + REACH
            total = row_product(row, nblocks, cols, counts, table, h)
            set_columns(out, i, first_value(row, total, onsite, field))
        return carry

    lax.fori_loop(0, count // unroll, step, 0)

    def rest(i, carry):
        fetch(lax.rem(i + local - REACH, local)).wait()
        return carry

    lax.fori_loop(0, 2 * REACH, rest, 0)


def first_edge(
    nblocks, local, cols, counts, onsite, near, far, field, h, out, near_out, far_out, table
):
    near_slot, far_slot = outer_slots(local)
    load_blocks(
        table,
        [
            (near, 0, near_slot, REACH),
            (far, 0, far_slot, REACH),
            (field, 0, REACH, 2 * REACH),
            (field, local - 2 * REACH, local - REACH, 2 * REACH),
        ],
    )
    unroll = 8

    def step(s, carry):
        for u in range(unroll):
            i = s * unroll + u
            row = jnp.where(i < REACH, i, i + local - 2 * REACH)
            total = row_product(row, nblocks, cols, counts, table, h)
            set_columns(out, i, first_value(row, total, onsite, field))
        return carry

    lax.fori_loop(0, 2 * REACH // unroll, step, 0)
    split_ends(out, near_out, far_out, REACH)


def second_value(row, total, onsite, first, field):
    diag = onsite[pl.ds(row, 1), :] - filter_center
    return 2.0 * (total + diag * first) / filter_half - columns(field, row)


def second_inner(nblocks, local, cols, counts, onsite, edge, inner, field, h, out, table):
    load_blocks(
        table,
        [
            (edge, 0, REACH, REACH),
            (inner, 0, 2 * REACH, local - 2 * REACH),
            (edge, REACH, local, REACH),
        ],
    )
    unroll = 8

    def step(s, carry):
        for u in range(unroll):
            i = s * unroll + u
            row = i + REACH
            total = row_product(row, nblocks, cols, counts, table, h)
            set_columns(out, i, second_value(row, total, onsite, columns(inner, i), field))
        return carry

    lax.fori_loop(0, (local - 2 * REACH) // unroll, step, 0)


def second_edge(
    nblocks, local, cols, counts, onsite, near, far, edge, inner, field, done, h, out, parts, table
):
    near_slot, far_slot = outer_slots(local)
    load_blocks(
        table,
        [
            (near, 0, near_slot, REACH),
            (far, 0, far_slot, REACH),
            (edge, 0, REACH, REACH),
            (inner, 0, 2 * REACH, REACH),
            (inner, local - 3 * REACH, local - REACH, REACH),
            (edge, REACH, local, REACH),
        ],
    )
    out[:, REACH * BLOCK : (local - REACH) * BLOCK] = done[...]
    unroll = 8

    def step(s, carry):
        for u in range(unroll):
            i = s * unroll + u
            row = jnp.where(i < REACH, i, i + local - 2 * REACH)
            total = row_product(row, nblocks, cols, counts, table, h)
            set_columns(out, row, second_value(row, total, onsite, columns(edge, i), field))
        return carry

    lax.fori_loop(0, 2 * REACH // unroll, step, 0)
    width = parts.shape[2]
    for k in range(parts.shape[0]):
        parts[k] = out[:, k * width : (k + 1) * width]


def gram(scale, parts, keep, give):
    groups, vcount, width = parts.shape
    total = groups * vcount
    a, b = halves(parts[...].reshape(total, width))
    both = (
        lax.dot_general(a, a, NT, preferred_element_type=f32)
        + lax.dot_general(a, b, NT, preferred_element_type=f32)
        + lax.dot_general(b, a, NT, preferred_element_type=f32)
    ) * scale
    low = both[:, : total // 2].reshape(groups, vcount, total // 2)
    high = both[:, total // 2 :].reshape(groups, vcount, total // 2)
    first = is_first_core()
    keep[...] = jnp.where(first, low, high)
    give[...] = jnp.where(first, high, low)


def join(side, terms, out):
    count, width = terms.shape[1:]
    for x in range(side):
        for core in range(2):
            total = None
            for y in range(side):
                one = terms[(x * side + y) * 2 + core]
                total = one if total is None else total + one
            out[x * count : (x + 1) * count, core * width : (core + 1) * width] = total


def params(mebibytes):
    return pltpu.CompilerParams(vmem_limit_bytes=mebibytes * 1024 * 1024)


def cost(rows, slots, vcount):
    return pl.CostEstimate(
        flops=rows * slots * BLOCK * BLOCK * vcount * 2 * 4,
        bytes_accessed=rows * slots * BLOCK * BLOCK * 4,
        transcendentals=0,
    )


def on_device(vectors, onsite, h_blocks, block_cols, block_counts):
    vcount, width = vectors.shape
    local, slots = block_cols.shape
    ranks = lax.axis_size("rows")
    groups = lax.axis_size("cols")
    nblocks = local * ranks
    reach = REACH * BLOCK
    edge_rows, inner_rows = 2 * REACH, local - 2 * REACH
    cols = block_cols.T
    onsite = onsite.reshape(local, BLOCK)

    def shape(*dims):
        return jax.ShapeDtypeStruct(dims, f32)

    table = pltpu.VMEM((local + 2 * REACH + 1, 2 * vcount, BLOCK), bf16)
    mate = [(i, i ^ 1) for i in range(ranks)]
    beyond = [(i, (i + 1 if i % 2 else i - 1) % ranks) for i in range(ranks)]

    def around(near, far):
        far = lax.ppermute(far, "rows", beyond)
        return lax.ppermute(near, "rows", mate), far

    def in_hbm(*arrays):
        return [pltpu.with_memory_space_constraint(x, pltpu.HBM) for x in arrays]

    near, far = pl.pallas_call(
        ends,
        in_specs=[HBM],
        out_specs=(VMEM, VMEM),
        out_shape=(pltpu.VMEM((vcount, reach), f32), pltpu.VMEM((vcount, reach), f32)),
        scratch_shapes=[pltpu.SemaphoreType.DMA((2,))],
        compiler_params=params(8),
        name="ends",
    )(*in_hbm(vectors))
    near, far = around(near, far)

    cols, counts, h, field, onsite, inner = pl.pallas_call(
        functools.partial(first_inner, nblocks, local),
        in_specs=[HBM] * 5,
        out_specs=(SMEM,) * 2 + (VMEM,) * 4,
        out_shape=(
            pltpu.SMEM(cols.shape, jnp.int32),
            pltpu.SMEM(block_counts.shape, jnp.int32),
            pltpu.VMEM(h_blocks.shape, f32),
            pltpu.VMEM(vectors.shape, f32),
            pltpu.VMEM(onsite.shape, f32),
            pltpu.VMEM((vcount, inner_rows * BLOCK), f32),
        ),
        scratch_shapes=[
            table,
            pltpu.SemaphoreType.DMA((local,)),
            pltpu.SemaphoreType.DMA((4,)),
        ],
        compiler_params=params(8),
        cost_estimate=cost(local, slots, vcount),
        name="first_inner",
    )(*in_hbm(cols, block_counts, onsite, vectors, h_blocks))

    edge, near, far = pl.pallas_call(
        functools.partial(first_edge, nblocks, local),
        in_specs=[SMEM, SMEM] + [VMEM] * 5,
        out_specs=(VMEM,) * 3,
        out_shape=(shape(vcount, 2 * reach), shape(vcount, reach), shape(vcount, reach)),
        scratch_shapes=[table],
        compiler_params=params(8),
        cost_estimate=cost(edge_rows, slots, vcount),
        name="first_edge",
    )(cols, counts, onsite, near, far, field, h)
    near, far = around(near, far)

    done = pl.pallas_call(
        functools.partial(second_inner, nblocks, local),
        in_specs=[SMEM, SMEM] + [VMEM] * 5,
        out_specs=VMEM,
        out_shape=shape(vcount, inner_rows * BLOCK),
        scratch_shapes=[table],
        compiler_params=params(8),
        cost_estimate=cost(inner_rows, slots, vcount),
        name="second_inner",
    )(cols, counts, onsite, edge, inner, field, h)

    filtered, parts = pl.pallas_call(
        functools.partial(second_edge, nblocks, local),
        in_specs=[SMEM, SMEM] + [VMEM] * 8,
        out_specs=(VMEM, VMEM),
        out_shape=(shape(vcount, width), shape(groups, vcount, width // groups)),
        scratch_shapes=[table],
        compiler_params=params(8),
        cost_estimate=cost(edge_rows, slots, vcount),
        name="second_edge",
    )(cols, counts, onsite, near, far, edge, inner, field, done, h)

    parts = lax.all_to_all(parts, "cols", 0, 0)
    total = vcount * groups
    keep, give = pl.pallas_call(
        functools.partial(gram, 1.0 / (width * ranks)),
        in_specs=[VMEM],
        out_specs=(VMEM, VMEM),
        out_shape=(shape(groups, vcount, total // 2), shape(groups, vcount, total // 2)),
        compiler_params=params(8),
        name="gram",
    )(parts)
    keep = keep + lax.ppermute(give, "rows", mate)

    side = 4
    share = vcount // side
    same = []
    for y in range(side):
        for core in range(2):
            at = [((x * side + y) * 2 + core) * groups for x in range(side)]
            same.append([r + z for z in range(groups) for r in at])
    terms = keep.reshape(groups * side, share, total // 2)
    terms = lax.all_to_all(terms, ("rows", "cols"), 0, 0, axis_index_groups=same)
    mine = jnp.sum(terms, axis=0)
    terms = lax.all_to_all(jnp.broadcast_to(mine[None], (ranks, *mine.shape)), "rows", 0, 0)
    correlation = pl.pallas_call(
        functools.partial(join, side),
        in_specs=[VMEM],
        out_specs=VMEM,
        out_shape=shape(vcount, total),
        compiler_params=params(8),
        name="join",
    )(terms)
    return (filtered, correlation)


def solution(mesh):
    return jax.shard_map(
        on_device,
        mesh=mesh,
        in_specs=(
            P("cols", "rows"),
            P("rows"),
            P("rows", None, None, None),
            P("rows", None),
            P("rows"),
        ),
        out_specs=(P("cols", "rows"), P("cols", None)),
        check_vma=False,
    )
```

```python
import functools

import jax
import jax.numpy as jnp
from jax import lax
from jax.experimental import pallas as pl
from jax.experimental.pallas import tpu as pltpu
from jax.sharding import PartitionSpec as P

REACH = 4
BLOCK = 128

filter_center = 1.0
filter_half = 2.0

f32, bf16 = jnp.float32, jnp.bfloat16
VMEM = pl.BlockSpec(memory_space=pltpu.VMEM)
SMEM = pl.BlockSpec(memory_space=pltpu.SMEM)
HBM = pl.BlockSpec(memory_space=pltpu.HBM)
NT = (((1,), (1,)), ((), ()))


def halves(x):
    high = x.astype(bf16)
    return high, (x - high.astype(f32)).astype(bf16)


def load_blocks(table, pieces):
    vcount = table.shape[1] // 2
    for ref, block, slot, blocks in pieces:
        for b in range(blocks):
            high, low = halves(ref[:, (block + b) * BLOCK : (block + b + 1) * BLOCK])
            table[slot + b, 0:vcount] = high
            table[slot + b, vcount : 2 * vcount] = low
    table[table.shape[0] - 1] = jnp.zeros(table.shape[1:], bf16)


def is_first_core():
    return lax.rem(lax.axis_index("rows"), 2) == 0


def outer_slots(local):
    first = is_first_core()
    return jnp.where(first, local + REACH, 0), jnp.where(first, 0, local + REACH)


def outer_end(ref, near):
    width = REACH * BLOCK
    high = ref.shape[1] - width
    start = jnp.where(is_first_core(), high, 0) if near else jnp.where(is_first_core(), 0, high)
    return ref.at[:, pl.ds(pl.multiple_of(start, BLOCK), width)]


def columns(ref, block):
    return ref[:, pl.ds(pl.multiple_of(block * BLOCK, BLOCK), BLOCK)]


def set_columns(ref, block, value):
    ref[:, pl.ds(pl.multiple_of(block * BLOCK, BLOCK), BLOCK)] = value


def row_product(row, nblocks, cols, counts, table, h):
    slots = h.shape[1]
    here = cols[0, row]
    used = counts[row]
    picked = []
    for k in range(slots):
        shift = cols[k, row] - here
        shift = jnp.where(shift > REACH, shift - nblocks, shift)
        shift = jnp.where(shift < -REACH, shift + nblocks, shift)
        picked.append(table[jnp.where(k < used, row + shift + REACH, table.shape[0] - 1)])
    left = jnp.concatenate(picked, axis=1)
    split = [halves(h[row, k]) for k in range(slots)]
    right = jnp.concatenate(
        [
            jnp.concatenate([high for high, _ in split], axis=1),
            jnp.concatenate([low for _, low in split], axis=1),
        ],
        axis=0,
    )
    both = lax.dot_general(left, right, NT, preferred_element_type=f32)
    v = left.shape[0] // 2
    return (both[:v, :BLOCK] + both[:v, BLOCK:]) + (both[v:, :BLOCK] + both[v:, BLOCK:])


def first_value(row, total, onsite, field):
    diag = onsite[pl.ds(row, 1), :] - filter_center
    return (total + diag * columns(field, row)) / filter_half


def far_end(field_hbm, far, sem):
    copy = pltpu.make_async_copy(outer_end(field_hbm, False), far, sem.at[0])
    copy.start()
    copy.wait()


def first_inner(
    nblocks, local, cols_hbm, counts_hbm, onsite_hbm, field_hbm, h_hbm,
    cols, counts, h, field, onsite, out, near_out, table, sems, small,
):
    count = local - 2 * REACH
    unroll = 4

    def fetch(row):
        return pltpu.make_async_copy(h_hbm.at[row], h.at[row], sems.at[row])

    copies = [
        pltpu.make_async_copy(a, b, small.at[n])
        for n, (a, b) in enumerate(
            [(field_hbm, field), (cols_hbm, cols), (counts_hbm, counts), (onsite_hbm, onsite)]
        )
    ]
    for copy in copies:
        copy.start()

    def begin(i, carry):
        fetch(lax.rem(i + REACH, local)).start()
        return carry

    lax.fori_loop(0, local, begin, 0)
    for copy in copies:
        copy.wait()
    near_out[...] = outer_end(field, True)[...]
    load_blocks(table, [(field, 0, REACH, local)])

    def step(s, carry):
        for u in range(unroll):
            fetch(s * unroll + u + REACH).wait()
        for u in range(unroll):
            i = s * unroll + u
            row = i + REACH
            total = row_product(row, nblocks, cols, counts, table, h)
            set_columns(out, i, first_value(row, total, onsite, field))
        return carry

    lax.fori_loop(0, count // unroll, step, 0)

    def rest(i, carry):
        fetch(lax.rem(i + local - REACH, local)).wait()
        return carry

    lax.fori_loop(0, 2 * REACH, rest, 0)


def first_edge(
    nblocks, local, cols, counts, onsite, near, far, field, h, out, far_out, table
):
    near_slot, far_slot = outer_slots(local)
    load_blocks(
        table,
        [
            (near, 0, near_slot, REACH),
            (far, 0, far_slot, REACH),
            (field, 0, REACH, 2 * REACH),
            (field, local - 2 * REACH, local - REACH, 2 * REACH),
        ],
    )
    unroll = 8

    def step(s, carry):
        for u in range(unroll):
            i = s * unroll + u
            row = jnp.where(i < REACH, i, i + local - 2 * REACH)
            total = row_product(row, nblocks, cols, counts, table, h)
            set_columns(out, i, first_value(row, total, onsite, field))
        return carry

    lax.fori_loop(0, 2 * REACH // unroll, step, 0)
    far_out[...] = outer_end(out, False)[...]


def second_value(row, total, onsite, first, field):
    diag = onsite[pl.ds(row, 1), :] - filter_center
    return 2.0 * (total + diag * first) / filter_half - columns(field, row)


def second_inner(
    nblocks, local, cols, counts, onsite, edge, inner, field, h, out, near_out, table
):
    near_out[...] = outer_end(edge, True)[...]
    load_blocks(
        table,
        [
            (edge, 0, REACH, REACH),
            (inner, 0, 2 * REACH, local - 2 * REACH),
            (edge, REACH, local, REACH),
        ],
    )
    unroll = 8

    def step(s, carry):
        for u in range(unroll):
            i = s * unroll + u
            row = i + REACH
            total = row_product(row, nblocks, cols, counts, table, h)
            set_columns(out, i, second_value(row, total, onsite, columns(inner, i), field))
        return carry

    lax.fori_loop(0, (local - 2 * REACH) // unroll, step, 0)


def second_edge(
    nblocks, local, cols, counts, onsite, near, far, edge, inner, field, done, h, out, parts, table
):
    near_slot, far_slot = outer_slots(local)
    load_blocks(
        table,
        [
            (near, 0, near_slot, REACH),
            (far, 0, far_slot, REACH),
            (edge, 0, REACH, REACH),
            (inner, 0, 2 * REACH, REACH),
            (inner, local - 3 * REACH, local - REACH, REACH),
            (edge, REACH, local, REACH),
        ],
    )
    out[:, REACH * BLOCK : (local - REACH) * BLOCK] = done[...]
    unroll = 8

    def step(s, carry):
        for u in range(unroll):
            i = s * unroll + u
            row = jnp.where(i < REACH, i, i + local - 2 * REACH)
            total = row_product(row, nblocks, cols, counts, table, h)
            set_columns(out, row, second_value(row, total, onsite, columns(edge, i), field))
        return carry

    lax.fori_loop(0, 2 * REACH // unroll, step, 0)
    width = parts.shape[2]
    for k in range(parts.shape[0]):
        parts[k] = out[:, k * width : (k + 1) * width]


def gram(scale, parts, keep, give):
    groups, vcount, width = parts.shape
    total = groups * vcount
    a, b = halves(parts[...].reshape(total, width))
    both = (
        lax.dot_general(a, a, NT, preferred_element_type=f32)
        + lax.dot_general(a, b, NT, preferred_element_type=f32)
        + lax.dot_general(b, a, NT, preferred_element_type=f32)
    ) * scale
    low = both[:, : total // 2].reshape(groups, vcount, total // 2)
    high = both[:, total // 2 :].reshape(groups, vcount, total // 2)
    first = is_first_core()
    keep[...] = jnp.where(first, low, high)
    give[...] = jnp.where(first, high, low)


def join(side, terms, out):
    count, width = terms.shape[1:]
    for x in range(side):
        for core in range(2):
            total = None
            for y in range(side):
                one = terms[(x * side + y) * 2 + core]
                total = one if total is None else total + one
            out[x * count : (x + 1) * count, core * width : (core + 1) * width] = total


def params(mebibytes):
    return pltpu.CompilerParams(vmem_limit_bytes=mebibytes * 1024 * 1024)


def cost(rows, slots, vcount):
    return pl.CostEstimate(
        flops=rows * slots * BLOCK * BLOCK * vcount * 2 * 4,
        bytes_accessed=rows * slots * BLOCK * BLOCK * 4,
        transcendentals=0,
    )


def on_device(vectors, onsite, h_blocks, block_cols, block_counts):
    vcount, width = vectors.shape
    local, slots = block_cols.shape
    ranks = lax.axis_size("rows")
    groups = lax.axis_size("cols")
    nblocks = local * ranks
    reach = REACH * BLOCK
    edge_rows, inner_rows = 2 * REACH, local - 2 * REACH
    cols = block_cols.T
    onsite = onsite.reshape(local, BLOCK)

    def shape(*dims):
        return jax.ShapeDtypeStruct(dims, f32)

    table = pltpu.VMEM((local + 2 * REACH + 1, 2 * vcount, BLOCK), bf16)
    mate = [(i, i ^ 1) for i in range(ranks)]
    beyond = [(i, (i + 1 if i % 2 else i - 1) % ranks) for i in range(ranks)]

    def in_hbm(*arrays):
        return [pltpu.with_memory_space_constraint(x, pltpu.HBM) for x in arrays]

    far = pl.pallas_call(
        far_end,
        in_specs=[HBM],
        out_specs=VMEM,
        out_shape=pltpu.VMEM((vcount, reach), f32),
        scratch_shapes=[pltpu.SemaphoreType.DMA((1,))],
        compiler_params=params(8),
        name="far_end",
    )(*in_hbm(vectors))
    far = lax.ppermute(far, "rows", beyond)

    cols, counts, h, field, onsite, inner, near = pl.pallas_call(
        functools.partial(first_inner, nblocks, local),
        in_specs=[HBM] * 5,
        out_specs=(SMEM,) * 2 + (VMEM,) * 5,
        out_shape=(
            pltpu.SMEM(cols.shape, jnp.int32),
            pltpu.SMEM(block_counts.shape, jnp.int32),
            pltpu.VMEM(h_blocks.shape, f32),
            pltpu.VMEM(vectors.shape, f32),
            pltpu.VMEM(onsite.shape, f32),
            pltpu.VMEM((vcount, inner_rows * BLOCK), f32),
            pltpu.VMEM((vcount, reach), f32),
        ),
        scratch_shapes=[
            table,
            pltpu.SemaphoreType.DMA((local,)),
            pltpu.SemaphoreType.DMA((4,)),
        ],
        compiler_params=params(8),
        cost_estimate=cost(local, slots, vcount),
        name="first_inner",
    )(*in_hbm(cols, block_counts, onsite, vectors, h_blocks))

    near = lax.ppermute(near, "rows", mate)

    edge, far = pl.pallas_call(
        functools.partial(first_edge, nblocks, local),
        in_specs=[SMEM, SMEM] + [VMEM] * 5,
        out_specs=(VMEM,) * 2,
        out_shape=(shape(vcount, 2 * reach), shape(vcount, reach)),
        scratch_shapes=[table],
        compiler_params=params(8),
        cost_estimate=cost(edge_rows, slots, vcount),
        name="first_edge",
    )(cols, counts, onsite, near, far, field, h)
    far = lax.ppermute(far, "rows", beyond)

    done, near = pl.pallas_call(
        functools.partial(second_inner, nblocks, local),
        in_specs=[SMEM, SMEM] + [VMEM] * 5,
        out_specs=(VMEM, VMEM),
        out_shape=(shape(vcount, inner_rows * BLOCK), shape(vcount, reach)),
        scratch_shapes=[table],
        compiler_params=params(8),
        cost_estimate=cost(inner_rows, slots, vcount),
        name="second_inner",
    )(cols, counts, onsite, edge, inner, field, h)

    near = lax.ppermute(near, "rows", mate)

    filtered, parts = pl.pallas_call(
        functools.partial(second_edge, nblocks, local),
        in_specs=[SMEM, SMEM] + [VMEM] * 8,
        out_specs=(VMEM, VMEM),
        out_shape=(shape(vcount, width), shape(groups, vcount, width // groups)),
        scratch_shapes=[table],
        compiler_params=params(8),
        cost_estimate=cost(edge_rows, slots, vcount),
        name="second_edge",
    )(cols, counts, onsite, near, far, edge, inner, field, done, h)

    parts = lax.all_to_all(parts, "cols", 0, 0)
    total = vcount * groups
    keep, give = pl.pallas_call(
        functools.partial(gram, 1.0 / (width * ranks)),
        in_specs=[VMEM],
        out_specs=(VMEM, VMEM),
        out_shape=(shape(groups, vcount, total // 2), shape(groups, vcount, total // 2)),
        compiler_params=params(8),
        name="gram",
    )(parts)
    keep = keep + lax.ppermute(give, "rows", mate)

    side = 4
    share = vcount // side
    same = []
    for y in range(side):
        for core in range(2):
            at = [((x * side + y) * 2 + core) * groups for x in range(side)]
            same.append([r + z for z in range(groups) for r in at])
    terms = keep.reshape(groups * side, share, total // 2)
    terms = lax.all_to_all(terms, ("rows", "cols"), 0, 0, axis_index_groups=same)
    mine = jnp.sum(terms, axis=0)
    terms = lax.all_to_all(jnp.broadcast_to(mine[None], (ranks, *mine.shape)), "rows", 0, 0)
    correlation = pl.pallas_call(
        functools.partial(join, side),
        in_specs=[VMEM],
        out_specs=VMEM,
        out_shape=shape(vcount, total),
        compiler_params=params(8),
        name="join",
    )(terms)
    return (filtered, correlation)


def solution(mesh):
    return jax.shard_map(
        on_device,
        mesh=mesh,
        in_specs=(
            P("cols", "rows"),
            P("rows"),
            P("rows", None, None, None),
            P("rows", None),
            P("rows"),
        ),
        out_specs=(P("cols", "rows"), P("cols", None)),
        check_vma=False,
    )
```

```python
import functools

import jax
import jax.numpy as jnp
from jax import lax
from jax.experimental import pallas as pl
from jax.experimental.pallas import tpu as pltpu
from jax.sharding import PartitionSpec as P

REACH = 4
BLOCK = 128

filter_center = 1.0
filter_half = 2.0

f32, bf16 = jnp.float32, jnp.bfloat16
VMEM = pl.BlockSpec(memory_space=pltpu.VMEM)
SMEM = pl.BlockSpec(memory_space=pltpu.SMEM)
HBM = pl.BlockSpec(memory_space=pltpu.HBM)
NT = (((1,), (1,)), ((), ()))


def halves(x):
    high = x.astype(bf16)
    return high, (x - high.astype(f32)).astype(bf16)


def load_blocks(table, pieces):
    vcount = table.shape[1] // 2
    for ref, block, slot, blocks in pieces:
        for b in range(blocks):
            high, low = halves(ref[:, (block + b) * BLOCK : (block + b + 1) * BLOCK])
            table[slot + b, 0:vcount] = high
            table[slot + b, vcount : 2 * vcount] = low
    table[table.shape[0] - 1] = jnp.zeros(table.shape[1:], bf16)


def is_first_core():
    return lax.rem(lax.axis_index("rows"), 2) == 0


def outer_slots(local):
    first = is_first_core()
    return jnp.where(first, local + REACH, 0), jnp.where(first, 0, local + REACH)


def split_ends(ref, near, far, count):
    width = count * BLOCK
    first = is_first_core()
    high = ref.shape[1] - width
    near[...] = ref[:, pl.ds(pl.multiple_of(jnp.where(first, high, 0), BLOCK), width)]
    far[...] = ref[:, pl.ds(pl.multiple_of(jnp.where(first, 0, high), BLOCK), width)]


def columns(ref, block):
    return ref[:, pl.ds(pl.multiple_of(block * BLOCK, BLOCK), BLOCK)]


def set_columns(ref, block, value):
    ref[:, pl.ds(pl.multiple_of(block * BLOCK, BLOCK), BLOCK)] = value


def row_product(row, nblocks, cols, counts, table, h):
    slots = h.shape[1]
    here = cols[0, row]
    used = counts[row]
    picked = []
    for k in range(slots):
        shift = cols[k, row] - here
        shift = jnp.where(shift > REACH, shift - nblocks, shift)
        shift = jnp.where(shift < -REACH, shift + nblocks, shift)
        picked.append(table[jnp.where(k < used, row + shift + REACH, table.shape[0] - 1)])
    left = jnp.concatenate(picked, axis=1)
    split = [halves(h[row, k]) for k in range(slots)]
    right = jnp.concatenate(
        [
            jnp.concatenate([high for high, _ in split], axis=1),
            jnp.concatenate([low for _, low in split], axis=1),
        ],
        axis=0,
    )
    both = lax.dot_general(left, right, NT, preferred_element_type=f32)
    v = left.shape[0] // 2
    return (both[:v, :BLOCK] + both[:v, BLOCK:]) + (both[v:, :BLOCK] + both[v:, BLOCK:])


def first_value(row, total, onsite, field):
    diag = onsite[pl.ds(row, 1), :] - filter_center
    return (total + diag * columns(field, row)) / filter_half


def ends(field_hbm, near, far, sems):
    width = near.shape[1]
    high = field_hbm.shape[1] - width
    first = is_first_core()
    copies = []
    for n, (start, ref) in enumerate(
        [(jnp.where(first, 0, high), far), (jnp.where(first, high, 0), near)]
    ):
        part = field_hbm.at[:, pl.ds(pl.multiple_of(start, BLOCK), width)]
        copies.append(pltpu.make_async_copy(part, ref, sems.at[n]))
    for copy in copies:
        copy.start()
    for copy in copies:
        copy.wait()


def first_inner(
    nblocks, local, cols_hbm, counts_hbm, onsite_hbm, field_hbm, h_hbm,
    cols, counts, h, field, onsite, out, table, sems, small,
):
    count = local - 2 * REACH
    unroll = 4

    def fetch(row):
        return pltpu.make_async_copy(h_hbm.at[row], h.at[row], sems.at[row])

    copies = [
        pltpu.make_async_copy(a, b, small.at[n])
        for n, (a, b) in enumerate(
            [(field_hbm, field), (cols_hbm, cols), (counts_hbm, counts), (onsite_hbm, onsite)]
        )
    ]
    for copy in copies:
        copy.start()

    def begin(i, carry):
        fetch(lax.rem(i + REACH, local)).start()
        return carry

    lax.fori_loop(0, local, begin, 0)
    for copy in copies:
        copy.wait()
    load_blocks(table, [(field, 0, REACH, local)])

    def step(s, carry):
        for u in range(unroll):
            fetch(s * unroll + u + REACH).wait()
        for u in range(unroll):
            i = s * unroll + u
            row = i + REACH
            total = row_product(row, nblocks, cols, counts, table, h)
            set_columns(out, i, first_value(row, total, onsite, field))
        return carry

    lax.fori_loop(0, count // unroll, step, 0)

    def rest(i, carry):
        fetch(lax.rem(i + local - REACH, local)).wait()
        return carry

    lax.fori_loop(0, 2 * REACH, rest, 0)


def first_edge(
    nblocks, local, cols, counts, onsite, near, far, field, h, out, near_out, far_out, table
):
    near_slot, far_slot = outer_slots(local)
    load_blocks(
        table,
        [
            (near, 0, near_slot, REACH),
            (far, 0, far_slot, REACH),
            (field, 0, REACH, 2 * REACH),
            (field, local - 2 * REACH, local - REACH, 2 * REACH),
        ],
    )
    unroll = 8

    def step(s, carry):
        for u in range(unroll):
            i = s * unroll + u
            row = jnp.where(i < REACH, i, i + local - 2 * REACH)
            total = row_product(row, nblocks, cols, counts, table, h)
            set_columns(out, i, first_value(row, total, onsite, field))
        return carry

    lax.fori_loop(0, 2 * REACH // unroll, step, 0)
    split_ends(out, near_out, far_out, REACH)


def second_value(row, total, onsite, first, field):
    diag = onsite[pl.ds(row, 1), :] - filter_center
    return 2.0 * (total + diag * first) / filter_half - columns(field, row)


def second_inner(nblocks, local, cols, counts, onsite, edge, inner, field, h, out, table):
    load_blocks(
        table,
        [
            (edge, 0, REACH, REACH),
            (inner, 0, 2 * REACH, local - 2 * REACH),
            (edge, REACH, local, REACH),
        ],
    )
    unroll = 8

    def step(s, carry):
        for u in range(unroll):
            i = s * unroll + u
            row = i + REACH
            total = row_product(row, nblocks, cols, counts, table, h)
            set_columns(out, i, second_value(row, total, onsite, columns(inner, i), field))
        return carry

    lax.fori_loop(0, (local - 2 * REACH) // unroll, step, 0)


def second_edge(
    nblocks, local, cols, counts, onsite, near, far, edge, inner, field, done, h, out, parts, table
):
    near_slot, far_slot = outer_slots(local)
    load_blocks(
        table,
        [
            (near, 0, near_slot, REACH),
            (far, 0, far_slot, REACH),
            (edge, 0, REACH, REACH),
            (inner, 0, 2 * REACH, REACH),
            (inner, local - 3 * REACH, local - REACH, REACH),
            (edge, REACH, local, REACH),
        ],
    )
    out[:, REACH * BLOCK : (local - REACH) * BLOCK] = done[...]
    unroll = 8

    def step(s, carry):
        for u in range(unroll):
            i = s * unroll + u
            row = jnp.where(i < REACH, i, i + local - 2 * REACH)
            total = row_product(row, nblocks, cols, counts, table, h)
            set_columns(out, row, second_value(row, total, onsite, columns(edge, i), field))
        return carry

    lax.fori_loop(0, 2 * REACH // unroll, step, 0)
    width = parts.shape[2]
    for k in range(parts.shape[0]):
        parts[k] = out[:, k * width : (k + 1) * width]


def gram(scale, parts, keep, give):
    groups, vcount, width = parts.shape
    total = groups * vcount
    a, b = halves(parts[...].reshape(total, width))
    both = (
        lax.dot_general(a, a, NT, preferred_element_type=f32)
        + lax.dot_general(a, b, NT, preferred_element_type=f32)
        + lax.dot_general(b, a, NT, preferred_element_type=f32)
    ) * scale
    low = both[:, : total // 2].reshape(groups, vcount, total // 2)
    high = both[:, total // 2 :].reshape(groups, vcount, total // 2)
    first = is_first_core()
    keep[...] = jnp.where(first, low, high)
    give[...] = jnp.where(first, high, low)


def join(side, terms, filtered, filtered_hbm, out_hbm, out, sems):
    write = pltpu.make_async_copy(filtered, filtered_hbm, sems.at[0])
    write.start()
    count, width = terms.shape[1:]
    for x in range(side):
        for core in range(2):
            total = None
            for y in range(side):
                one = terms[(x * side + y) * 2 + core]
                total = one if total is None else total + one
            out[x * count : (x + 1) * count, core * width : (core + 1) * width] = total
    last = pltpu.make_async_copy(out, out_hbm, sems.at[1])
    last.start()
    write.wait()
    last.wait()


def params(mebibytes):
    return pltpu.CompilerParams(vmem_limit_bytes=mebibytes * 1024 * 1024)


def cost(rows, slots, vcount):
    return pl.CostEstimate(
        flops=rows * slots * BLOCK * BLOCK * vcount * 2 * 4,
        bytes_accessed=rows * slots * BLOCK * BLOCK * 4,
        transcendentals=0,
    )


def on_device(vectors, onsite, h_blocks, block_cols, block_counts):
    vcount, width = vectors.shape
    local, slots = block_cols.shape
    ranks = lax.axis_size("rows")
    groups = lax.axis_size("cols")
    nblocks = local * ranks
    reach = REACH * BLOCK
    edge_rows, inner_rows = 2 * REACH, local - 2 * REACH
    cols = block_cols.T
    onsite = onsite.reshape(local, BLOCK)

    def shape(*dims):
        return jax.ShapeDtypeStruct(dims, f32)

    table = pltpu.VMEM((local + 2 * REACH + 1, 2 * vcount, BLOCK), bf16)
    mate = [(i, i ^ 1) for i in range(ranks)]
    beyond = [(i, (i + 1 if i % 2 else i - 1) % ranks) for i in range(ranks)]

    def around(near, far):
        far = lax.ppermute(far, "rows", beyond)
        return lax.ppermute(near, "rows", mate), far

    def in_hbm(*arrays):
        return [pltpu.with_memory_space_constraint(x, pltpu.HBM) for x in arrays]

    near, far = pl.pallas_call(
        ends,
        in_specs=[HBM],
        out_specs=(VMEM, VMEM),
        out_shape=(pltpu.VMEM((vcount, reach), f32), pltpu.VMEM((vcount, reach), f32)),
        scratch_shapes=[pltpu.SemaphoreType.DMA((2,))],
        compiler_params=params(8),
        name="ends",
    )(*in_hbm(vectors))
    near, far = around(near, far)

    cols, counts, h, field, onsite, inner = pl.pallas_call(
        functools.partial(first_inner, nblocks, local),
        in_specs=[HBM] * 5,
        out_specs=(SMEM,) * 2 + (VMEM,) * 4,
        out_shape=(
            pltpu.SMEM(cols.shape, jnp.int32),
            pltpu.SMEM(block_counts.shape, jnp.int32),
            pltpu.VMEM(h_blocks.shape, f32),
            pltpu.VMEM(vectors.shape, f32),
            pltpu.VMEM(onsite.shape, f32),
            pltpu.VMEM((vcount, inner_rows * BLOCK), f32),
        ),
        scratch_shapes=[
            table,
            pltpu.SemaphoreType.DMA((local,)),
            pltpu.SemaphoreType.DMA((4,)),
        ],
        compiler_params=params(8),
        cost_estimate=cost(local, slots, vcount),
        name="first_inner",
    )(*in_hbm(cols, block_counts, onsite, vectors, h_blocks))

    edge, near, far = pl.pallas_call(
        functools.partial(first_edge, nblocks, local),
        in_specs=[SMEM, SMEM] + [VMEM] * 5,
        out_specs=(VMEM,) * 3,
        out_shape=(shape(vcount, 2 * reach), shape(vcount, reach), shape(vcount, reach)),
        scratch_shapes=[table],
        compiler_params=params(8),
        cost_estimate=cost(edge_rows, slots, vcount),
        name="first_edge",
    )(cols, counts, onsite, near, far, field, h)
    near, far = around(near, far)

    done = pl.pallas_call(
        functools.partial(second_inner, nblocks, local),
        in_specs=[SMEM, SMEM] + [VMEM] * 5,
        out_specs=VMEM,
        out_shape=shape(vcount, inner_rows * BLOCK),
        scratch_shapes=[table],
        compiler_params=params(8),
        cost_estimate=cost(inner_rows, slots, vcount),
        name="second_inner",
    )(cols, counts, onsite, edge, inner, field, h)

    filtered, parts = pl.pallas_call(
        functools.partial(second_edge, nblocks, local),
        in_specs=[SMEM, SMEM] + [VMEM] * 8,
        out_specs=(VMEM, VMEM),
        out_shape=(
            pltpu.VMEM((vcount, width), f32),
            shape(groups, vcount, width // groups),
        ),
        scratch_shapes=[table],
        compiler_params=params(8),
        cost_estimate=cost(edge_rows, slots, vcount),
        name="second_edge",
    )(cols, counts, onsite, near, far, edge, inner, field, done, h)

    parts = lax.all_to_all(parts, "cols", 0, 0)
    total = vcount * groups
    keep, give = pl.pallas_call(
        functools.partial(gram, 1.0 / (width * ranks)),
        in_specs=[VMEM],
        out_specs=(VMEM, VMEM),
        out_shape=(shape(groups, vcount, total // 2), shape(groups, vcount, total // 2)),
        compiler_params=params(8),
        name="gram",
    )(parts)
    keep = keep + lax.ppermute(give, "rows", mate)

    side = 4
    share = vcount // side
    same = []
    for y in range(side):
        for core in range(2):
            at = [((x * side + y) * 2 + core) * groups for x in range(side)]
            same.append([r + z for z in range(groups) for r in at])
    terms = keep.reshape(groups * side, share, total // 2)
    terms = lax.all_to_all(terms, ("rows", "cols"), 0, 0, axis_index_groups=same)
    mine = jnp.sum(terms, axis=0)
    terms = lax.all_to_all(jnp.broadcast_to(mine[None], (ranks, *mine.shape)), "rows", 0, 0)
    filtered, correlation = pl.pallas_call(
        functools.partial(join, side),
        in_specs=[VMEM, VMEM],
        out_specs=(HBM, HBM),
        out_shape=(shape(vcount, width), shape(vcount, total)),
        scratch_shapes=[pltpu.VMEM((vcount, total), f32), pltpu.SemaphoreType.DMA((2,))],
        compiler_params=params(8),
        name="join",
    )(terms, filtered)
    return (filtered, correlation)


def solution(mesh):
    return jax.shard_map(
        on_device,
        mesh=mesh,
        in_specs=(
            P("cols", "rows"),
            P("rows"),
            P("rows", None, None, None),
            P("rows", None),
            P("rows"),
        ),
        out_specs=(P("cols", "rows"), P("cols", None)),
        check_vma=False,
    )
```

```python
import functools

import jax
import jax.numpy as jnp
from jax import lax
from jax.experimental import pallas as pl
from jax.experimental.pallas import tpu as pltpu
from jax.sharding import PartitionSpec as P

REACH = 4
BLOCK = 128

filter_center = 1.0
filter_half = 2.0

f32, bf16 = jnp.float32, jnp.bfloat16
VMEM = pl.BlockSpec(memory_space=pltpu.VMEM)
SMEM = pl.BlockSpec(memory_space=pltpu.SMEM)
HBM = pl.BlockSpec(memory_space=pltpu.HBM)
NT = (((1,), (1,)), ((), ()))


def halves(x):
    high = x.astype(bf16)
    return high, (x - high.astype(f32)).astype(bf16)


def load_blocks(table, pieces):
    vcount = table.shape[1] // 2
    for ref, block, slot, blocks in pieces:
        for b in range(blocks):
            high, low = halves(ref[:, (block + b) * BLOCK : (block + b + 1) * BLOCK])
            table[slot + b, 0:vcount] = high
            table[slot + b, vcount : 2 * vcount] = low
    table[table.shape[0] - 1] = jnp.zeros(table.shape[1:], bf16)


def is_first_core():
    return lax.rem(lax.axis_index("rows"), 2) == 0


def outer_slots(local):
    first = is_first_core()
    return jnp.where(first, local + REACH, 0), jnp.where(first, 0, local + REACH)


def split_ends(ref, near, far, count):
    width = count * BLOCK
    first = is_first_core()
    high = ref.shape[1] - width
    near[...] = ref[:, pl.ds(pl.multiple_of(jnp.where(first, high, 0), BLOCK), width)]
    far[...] = ref[:, pl.ds(pl.multiple_of(jnp.where(first, 0, high), BLOCK), width)]


def columns(ref, block):
    return ref[:, pl.ds(pl.multiple_of(block * BLOCK, BLOCK), BLOCK)]


def set_columns(ref, block, value):
    ref[:, pl.ds(pl.multiple_of(block * BLOCK, BLOCK), BLOCK)] = value


def row_product(row, nblocks, cols, counts, table, h):
    slots = h.shape[1]
    here = cols[0, row]
    used = counts[row]
    picked = []
    for k in range(slots):
        shift = cols[k, row] - here
        shift = jnp.where(shift > REACH, shift - nblocks, shift)
        shift = jnp.where(shift < -REACH, shift + nblocks, shift)
        picked.append(table[jnp.where(k < used, row + shift + REACH, table.shape[0] - 1)])
    left = jnp.concatenate(picked, axis=1)
    split = [halves(h[row, k]) for k in range(slots)]
    right = jnp.concatenate(
        [
            jnp.concatenate([high for high, _ in split], axis=1),
            jnp.concatenate([low for _, low in split], axis=1),
        ],
        axis=0,
    )
    both = lax.dot_general(left, right, NT, preferred_element_type=f32)
    v = left.shape[0] // 2
    return (both[:v, :BLOCK] + both[:v, BLOCK:]) + (both[v:, :BLOCK] + both[v:, BLOCK:])


def first_value(row, total, onsite, field):
    diag = onsite[pl.ds(row, 1), :] - filter_center
    return (total + diag * columns(field, row)) / filter_half


def ends(field_hbm, near, far, sems):
    width = near.shape[1]
    high = field_hbm.shape[1] - width
    first = is_first_core()
    copies = []
    for n, (start, ref) in enumerate(
        [(jnp.where(first, 0, high), far), (jnp.where(first, high, 0), near)]
    ):
        part = field_hbm.at[:, pl.ds(pl.multiple_of(start, BLOCK), width)]
        copies.append(pltpu.make_async_copy(part, ref, sems.at[n]))
    for copy in copies:
        copy.start()
    for copy in copies:
        copy.wait()


def first_inner(
    nblocks, local, cols_hbm, counts_hbm, onsite_hbm, field_hbm, h_hbm,
    cols, counts, h, field, onsite, out, table, sems, small,
):
    count = local - 2 * REACH
    unroll = 4

    def fetch(row):
        return pltpu.make_async_copy(h_hbm.at[row], h.at[row], sems.at[row])

    copies = [
        pltpu.make_async_copy(a, b, small.at[n])
        for n, (a, b) in enumerate(
            [(field_hbm, field), (cols_hbm, cols), (counts_hbm, counts), (onsite_hbm, onsite)]
        )
    ]
    for copy in copies:
        copy.start()

    def begin(i, carry):
        fetch(lax.rem(i + REACH, local)).start()
        return carry

    lax.fori_loop(0, local, begin, 0)
    for copy in copies:
        copy.wait()
    load_blocks(table, [(field, 0, REACH, local)])

    def step(s, carry):
        for u in range(unroll):
            fetch(s * unroll + u + REACH).wait()
        for u in range(unroll):
            i = s * unroll + u
            row = i + REACH
            total = row_product(row, nblocks, cols, counts, table, h)
            set_columns(out, i, first_value(row, total, onsite, field))
        return carry

    lax.fori_loop(0, count // unroll, step, 0)

    def rest(i, carry):
        fetch(lax.rem(i + local - REACH, local)).wait()
        return carry

    lax.fori_loop(0, 2 * REACH, rest, 0)


def first_edge(
    nblocks, local, cols, counts, onsite, near, far, field, h, out, near_out, far_out, table
):
    near_slot, far_slot = outer_slots(local)
    load_blocks(
        table,
        [
            (near, 0, near_slot, REACH),
            (far, 0, far_slot, REACH),
            (field, 0, REACH, 2 * REACH),
            (field, local - 2 * REACH, local - REACH, 2 * REACH),
        ],
    )
    unroll = 8

    def step(s, carry):
        for u in range(unroll):
            i = s * unroll + u
            row = jnp.where(i < REACH, i, i + local - 2 * REACH)
            total = row_product(row, nblocks, cols, counts, table, h)
            set_columns(out, i, first_value(row, total, onsite, field))
        return carry

    lax.fori_loop(0, 2 * REACH // unroll, step, 0)
    split_ends(out, near_out, far_out, REACH)


def second_value(row, total, onsite, first, field):
    diag = onsite[pl.ds(row, 1), :] - filter_center
    return 2.0 * (total + diag * first) / filter_half - columns(field, row)


def second_inner(nblocks, local, cols, counts, onsite, edge, inner, field, h, out, table):
    load_blocks(
        table,
        [
            (edge, 0, REACH, REACH),
            (inner, 0, 2 * REACH, local - 2 * REACH),
            (edge, REACH, local, REACH),
        ],
    )
    unroll = 24

    def step(s, carry):
        for u in range(unroll):
            i = s * unroll + u
            row = i + REACH
            total = row_product(row, nblocks, cols, counts, table, h)
            set_columns(out, i, second_value(row, total, onsite, columns(inner, i), field))
        return carry

    lax.fori_loop(0, (local - 2 * REACH) // unroll, step, 0)


def second_edge(
    nblocks, local, cols, counts, onsite, near, far, edge, inner, field, done, h, out, parts, table
):
    near_slot, far_slot = outer_slots(local)
    load_blocks(
        table,
        [
            (near, 0, near_slot, REACH),
            (far, 0, far_slot, REACH),
            (edge, 0, REACH, REACH),
            (inner, 0, 2 * REACH, REACH),
            (inner, local - 3 * REACH, local - REACH, REACH),
            (edge, REACH, local, REACH),
        ],
    )
    out[:, REACH * BLOCK : (local - REACH) * BLOCK] = done[...]
    unroll = 8

    def step(s, carry):
        for u in range(unroll):
            i = s * unroll + u
            row = jnp.where(i < REACH, i, i + local - 2 * REACH)
            total = row_product(row, nblocks, cols, counts, table, h)
            set_columns(out, row, second_value(row, total, onsite, columns(edge, i), field))
        return carry

    lax.fori_loop(0, 2 * REACH // unroll, step, 0)
    width = parts.shape[2]
    for k in range(parts.shape[0]):
        parts[k] = out[:, k * width : (k + 1) * width]


def gram(scale, parts, keep, give):
    groups, vcount, width = parts.shape
    total = groups * vcount
    a, b = halves(parts[...].reshape(total, width))
    both = (
        lax.dot_general(a, a, NT, preferred_element_type=f32)
        + lax.dot_general(a, b, NT, preferred_element_type=f32)
        + lax.dot_general(b, a, NT, preferred_element_type=f32)
    ) * scale
    low = both[:, : total // 2].reshape(groups, vcount, total // 2)
    high = both[:, total // 2 :].reshape(groups, vcount, total // 2)
    first = is_first_core()
    keep[...] = jnp.where(first, low, high)
    give[...] = jnp.where(first, high, low)


def join(side, terms, filtered, filtered_hbm, out_hbm, out, sems):
    write = pltpu.make_async_copy(filtered, filtered_hbm, sems.at[0])
    write.start()
    count, width = terms.shape[1:]
    for x in range(side):
        for core in range(2):
            total = None
            for y in range(side):
                one = terms[(x * side + y) * 2 + core]
                total = one if total is None else total + one
            out[x * count : (x + 1) * count, core * width : (core + 1) * width] = total
    last = pltpu.make_async_copy(out, out_hbm, sems.at[1])
    last.start()
    write.wait()
    last.wait()


def params(mebibytes):
    return pltpu.CompilerParams(vmem_limit_bytes=mebibytes * 1024 * 1024)


def cost(rows, slots, vcount):
    return pl.CostEstimate(
        flops=rows * slots * BLOCK * BLOCK * vcount * 2 * 4,
        bytes_accessed=rows * slots * BLOCK * BLOCK * 4,
        transcendentals=0,
    )


def on_device(vectors, onsite, h_blocks, block_cols, block_counts):
    vcount, width = vectors.shape
    local, slots = block_cols.shape
    ranks = lax.axis_size("rows")
    groups = lax.axis_size("cols")
    nblocks = local * ranks
    reach = REACH * BLOCK
    edge_rows, inner_rows = 2 * REACH, local - 2 * REACH
    cols = block_cols.T
    onsite = onsite.reshape(local, BLOCK)

    def shape(*dims):
        return jax.ShapeDtypeStruct(dims, f32)

    table = pltpu.VMEM((local + 2 * REACH + 1, 2 * vcount, BLOCK), bf16)
    mate = [(i, i ^ 1) for i in range(ranks)]
    beyond = [(i, (i + 1 if i % 2 else i - 1) % ranks) for i in range(ranks)]

    def around(near, far):
        far = lax.ppermute(far, "rows", beyond)
        return lax.ppermute(near, "rows", mate), far

    def in_hbm(*arrays):
        return [pltpu.with_memory_space_constraint(x, pltpu.HBM) for x in arrays]

    near, far = pl.pallas_call(
        ends,
        in_specs=[HBM],
        out_specs=(VMEM, VMEM),
        out_shape=(pltpu.VMEM((vcount, reach), f32), pltpu.VMEM((vcount, reach), f32)),
        scratch_shapes=[pltpu.SemaphoreType.DMA((2,))],
        compiler_params=params(8),
        name="ends",
    )(*in_hbm(vectors))
    near, far = around(near, far)

    cols, counts, h, field, onsite, inner = pl.pallas_call(
        functools.partial(first_inner, nblocks, local),
        in_specs=[HBM] * 5,
        out_specs=(SMEM,) * 2 + (VMEM,) * 4,
        out_shape=(
            pltpu.SMEM(cols.shape, jnp.int32),
            pltpu.SMEM(block_counts.shape, jnp.int32),
            pltpu.VMEM(h_blocks.shape, f32),
            pltpu.VMEM(vectors.shape, f32),
            pltpu.VMEM(onsite.shape, f32),
            pltpu.VMEM((vcount, inner_rows * BLOCK), f32),
        ),
        scratch_shapes=[
            table,
            pltpu.SemaphoreType.DMA((local,)),
            pltpu.SemaphoreType.DMA((4,)),
        ],
        compiler_params=params(8),
        cost_estimate=cost(local, slots, vcount),
        name="first_inner",
    )(*in_hbm(cols, block_counts, onsite, vectors, h_blocks))

    edge, near, far = pl.pallas_call(
        functools.partial(first_edge, nblocks, local),
        in_specs=[SMEM, SMEM] + [VMEM] * 5,
        out_specs=(VMEM,) * 3,
        out_shape=(shape(vcount, 2 * reach), shape(vcount, reach), shape(vcount, reach)),
        scratch_shapes=[table],
        compiler_params=params(8),
        cost_estimate=cost(edge_rows, slots, vcount),
        name="first_edge",
    )(cols, counts, onsite, near, far, field, h)
    near, far = around(near, far)

    done = pl.pallas_call(
        functools.partial(second_inner, nblocks, local),
        in_specs=[SMEM, SMEM] + [VMEM] * 5,
        out_specs=VMEM,
        out_shape=shape(vcount, inner_rows * BLOCK),
        scratch_shapes=[table],
        compiler_params=params(8),
        cost_estimate=cost(inner_rows, slots, vcount),
        name="second_inner",
    )(cols, counts, onsite, edge, inner, field, h)

    filtered, parts = pl.pallas_call(
        functools.partial(second_edge, nblocks, local),
        in_specs=[SMEM, SMEM] + [VMEM] * 8,
        out_specs=(VMEM, VMEM),
        out_shape=(
            pltpu.VMEM((vcount, width), f32),
            shape(groups, vcount, width // groups),
        ),
        scratch_shapes=[table],
        compiler_params=params(8),
        cost_estimate=cost(edge_rows, slots, vcount),
        name="second_edge",
    )(cols, counts, onsite, near, far, edge, inner, field, done, h)

    parts = lax.all_to_all(parts, "cols", 0, 0)
    total = vcount * groups
    keep, give = pl.pallas_call(
        functools.partial(gram, 1.0 / (width * ranks)),
        in_specs=[VMEM],
        out_specs=(VMEM, VMEM),
        out_shape=(shape(groups, vcount, total // 2), shape(groups, vcount, total // 2)),
        compiler_params=params(8),
        name="gram",
    )(parts)
    keep = keep + lax.ppermute(give, "rows", mate)

    side = 4
    share = vcount // side
    same = []
    for y in range(side):
        for core in range(2):
            at = [((x * side + y) * 2 + core) * groups for x in range(side)]
            same.append([r + z for z in range(groups) for r in at])
    terms = keep.reshape(groups * side, share, total // 2)
    terms = lax.all_to_all(terms, ("rows", "cols"), 0, 0, axis_index_groups=same)
    mine = jnp.sum(terms, axis=0)
    terms = lax.all_to_all(jnp.broadcast_to(mine[None], (ranks, *mine.shape)), "rows", 0, 0)
    filtered, correlation = pl.pallas_call(
        functools.partial(join, side),
        in_specs=[VMEM, VMEM],
        out_specs=(HBM, HBM),
        out_shape=(shape(vcount, width), shape(vcount, total)),
        scratch_shapes=[pltpu.VMEM((vcount, total), f32), pltpu.SemaphoreType.DMA((2,))],
        compiler_params=params(8),
        name="join",
    )(terms, filtered)
    return (filtered, correlation)


def solution(mesh):
    return jax.shard_map(
        on_device,
        mesh=mesh,
        in_specs=(
            P("cols", "rows"),
            P("rows"),
            P("rows", None, None, None),
            P("rows", None),
            P("rows"),
        ),
        out_specs=(P("cols", "rows"), P("cols", None)),
        check_vma=False,
    )
```
